256 devices in a mesh: blk: 32 (over z, y_lo, core), group: 8 (over y_hi, x).
Axes of the slice: x: 4, y: 4 (y_hi: 2, y_lo: 2; y = y_hi * 2 + y_lo), z: 8, core: 2. Of those that a mesh axis runs over, the one named last changes fastest.
Arguments:
- picture_embedding_matrix: float32 [32768, 1152], P(('blk', 'group')), may hold values from -4 to 4
- caption_embedding_matrix: float32 [32768, 1152], P(('blk', 'group')), may hold values from -4 to 4
- inverse_softness: float32 [1], replicated, may hold values from 8 to 12
- similarity_offset: float32 [1], replicated, may hold values from -4 to -2
Outputs:
- image_grad: float32 [32768, 1152], P(('blk', 'group'))
- text_gradient: float32 [32768, 1152], P(('blk', 'group'))
The draws below stay inside these ranges and needn't reach their ends.
All inputs are finite; a program needn't handle non-finite values.
Results may differ from the reference program's by a relative error of at most 0.004.
Values may be sent and summed in bfloat16 or wider, within the bound.
A program may use at most 64 MiB of HBM per device.

```python
import math
import jax
import jax.numpy as jnp
from jax import lax

D = 1152
PAIRS_DEV = 128
PAIRS = 32768
REACH = 7
N_BLK = 32
N_GROUP = 8


def spread_rows(key):
    key_row, key_col, key_norm = jax.random.split(key, 3)
    row_factor_scale = jnp.exp(jax.random.uniform(key_row, (PAIRS, 1), jnp.float32, 0.0, math.log(10.0)))
    col_scale = jnp.exp(jax.random.uniform(key_col, (1, D), jnp.float32, 0.0, math.log(10.0)))
    base = jax.random.truncated_normal(key_norm, -4.0, 4.0, (PAIRS, D), jnp.float32)
    return base * row_factor_scale * col_scale / 125.0


def draw_picture_embedding_matrix(key, part):
    key = jax.random.fold_in(key, 11)
    return spread_rows(key)


def draw_caption_embedding_matrix(key, part):
    key = jax.random.fold_in(key, 23)
    return spread_rows(key)


def setup_inputs(seed: int = 0) -> dict:
    keys = jax.random.split(jax.random.key(seed), 5)
    picture_embedding_matrix = draw_picture_embedding_matrix(jax.random.fold_in(keys[4], 71), 0)
    caption_embedding_matrix = draw_caption_embedding_matrix(jax.random.fold_in(keys[4], 71), 0)
    inverse_softness = jnp.clip(jax.random.uniform(keys[2], (1,), jnp.float32, 8.0, 12.0), 8.0, 12.0)
    similarity_offset = jnp.clip(jax.random.uniform(keys[3], (1,), jnp.float32, -4.0, -2.0), -4.0, -2.0)
    return {"picture_embedding_matrix": picture_embedding_matrix, "caption_embedding_matrix": caption_embedding_matrix, "inverse_softness": inverse_softness, "similarity_offset": similarity_offset}


EPS = 1e-06

def unit_rows(embed):
    inverse = lax.rsqrt(lax.optimization_barrier(jnp.sum(embed * embed, axis=1, keepdims=True)) + EPS)
    return (embed * inverse, inverse)

def reference(picture_embedding_matrix, caption_embedding_matrix, inverse_softness, similarity_offset):
    normed_picture_matrix, inv_image = unit_rows(picture_embedding_matrix)
    unit_text, inv_text = unit_rows(caption_embedding_matrix)
    image_bf = normed_picture_matrix.astype(jnp.bfloat16)
    caption_halfprecision = unit_text.astype(jnp.bfloat16)
    similarity_multiplier = inverse_softness[0]
    offset = similarity_offset[0]
    block_rows = PAIRS_DEV * N_GROUP
    diagonal = jnp.eye(block_rows, dtype=jnp.float32)

    def visit(text_dir, index):
        start = (index * block_rows).astype(jnp.int32)
        block = lax.dynamic_slice_in_dim(image_bf, start, block_rows, 0)
        image_part = jnp.zeros((block_rows, D), jnp.float32)
        for dist in range(-REACH, REACH + 1):
            text_start_row = ((index + dist) % N_BLK * block_rows).astype(jnp.int32)
            texts = lax.dynamic_slice_in_dim(caption_halfprecision, text_start_row, block_rows, 0)
            logits = jnp.dot(block, texts.T, preferred_element_type=jnp.float32) * similarity_multiplier + offset
            target = diagonal if dist == 0 else jnp.zeros_like(diagonal)
            coeff = (similarity_multiplier * (jax.nn.sigmoid(logits) - target)).astype(jnp.bfloat16)
            image_part = image_part + jnp.dot(coeff, texts, preferred_element_type=jnp.float32)
            update = jnp.dot(coeff.T, block, preferred_element_type=jnp.float32)
            former = lax.dynamic_slice_in_dim(text_dir, text_start_row, block_rows, 0)
            text_dir = lax.dynamic_update_slice_in_dim(text_dir, former + update, text_start_row, 0)
        return (text_dir, image_part)
    text_dir, parts = lax.scan(visit, jnp.zeros((PAIRS, D), jnp.float32), jnp.arange(N_BLK, dtype=jnp.int32))
    image_dir = parts.reshape(PAIRS, D)
    image_grad = (image_dir - normed_picture_matrix * lax.optimization_barrier(jnp.sum(normed_picture_matrix * image_dir, axis=1, keepdims=True))) * inv_image
    text_gradient = (text_dir - unit_text * lax.optimization_barrier(jnp.sum(unit_text * text_dir, axis=1, keepdims=True))) * inv_text
    return (image_grad, text_gradient)
```

```python
import functools

import jax
import jax.numpy as jnp
from jax import lax
from jax.experimental import pallas as pl
from jax.experimental.pallas import tpu as pltpu
from jax.sharding import PartitionSpec as P

EPS = 1e-06
F32 = jnp.float32
BF16 = jnp.bfloat16

OWN, BEHIND, AHEAD, FAR = range(4)

IMG_Y, IMG_CORE, IMG_CORE_Y = 0, 1, 2
IMG_UP, IMG_DOWN, IMG_UP_Y, IMG_DOWN_Y = 3, 4, 5, 6
IMG_BEHIND_CORE, IMG_BEHIND_CORE_Y, IMG_AHEAD_CORE, IMG_AHEAD_CORE_Y = 7, 8, 9, 10
IMG_FAR_CORE, IMG_FAR_Y, IMG_FAR_CORE_Y = 11, 12, 13
TXT_Y = 14
TXT_RIGHT, TXT_LEFT, TXT_RIGHT2, TXT_LEFT2 = 15, 17, 19, 21
BACK = 23


def unit_rows(embed):
    inverse = lax.rsqrt(jnp.sum(embed * embed, axis=1, keepdims=True) + EPS)
    return embed * inverse, inverse


def kernel(
    scale_ref,
    offset_ref,
    image_ref,
    text_ref,
    image_grad_ref,
    text_grad_ref,
    imgs,
    txts,
    image_sum,
    text_sum,
    coeff_buf,
    coeff_t_buf,
    image_out,
    image_in,
    text_out,
    text_in,
    send_sem,
    recv_sem,
):
    rows, width = image_ref.shape
    half = rows // 2
    n_blk = lax.axis_size("blk")
    blk = lax.axis_index("blk")
    group = lax.axis_index("group")
    core = blk % 2
    y = (blk // 2) % 2

    def device(dz=0, flip=0, dx=0, flip_y=0):
        plane = (blk // 4 + dz + n_blk // 4) % (n_blk // 4)
        within = blk % 4
        if flip % 2:
            within = within + 1 - 2 * core
        if flip // 2:
            within = within + 2 - 4 * y
        x = (group % 4 + dx + 4) % 4
        upper = group // 4
        if flip_y:
            upper = 1 - upper
        return (plane * 4 + within, upper * 4 + x)

    mate = device(flip=1)
    y_near = device(flip=2)
    up, down = device(dz=1), device(dz=-1)
    cross = device(dz=2 * core - 1, flip=1)
    far_to = device(dz=1 - 2 * y)
    far_home = device(dz=2 * y - 1)
    right, left = device(dx=1), device(dx=-1)
    y_far = device(flip_y=1)
    cross_group = 2 - core
    far_group = 1 + y

    barrier = pltpu.get_barrier_semaphore()
    for partner in (mate, y_near, up, down, cross, right, left, y_far):
        pl.semaphore_signal(barrier, inc=1, device_id=partner, device_id_type=pl.DeviceIdType.MESH)

    def message(index, source, target, to):
        return pltpu.make_async_remote_copy(
            src_ref=source,
            dst_ref=target,
            send_sem=send_sem.at[index],
            recv_sem=recv_sem.at[index],
            device_id=to,
            device_id_type=pl.DeviceIdType.MESH,
        )

    def slot(k):
        return pl.ds(k * rows, rows)

    def img(g, k):
        return imgs.at[g, slot(k)]

    def txt(h, k):
        return txts.at[h, slot(k)]

    upper_part, lower_part = pl.ds(2 * rows, half), pl.ds(2 * rows + half, half)

    gather = {
        IMG_Y: (img(OWN, 0), img(OWN, 2), y_near),
        IMG_CORE: (img(OWN, 0), img(OWN, 1), mate),
        IMG_CORE_Y: (img(OWN, 2), img(OWN, 3), mate),
        IMG_UP: (img(OWN, 0), img(BEHIND, 0), up),
        IMG_DOWN: (img(OWN, 0), img(AHEAD, 0), down),
        IMG_UP_Y: (img(OWN, 2), img(BEHIND, 2), up),
        IMG_DOWN_Y: (img(OWN, 2), img(AHEAD, 2), down),
        IMG_BEHIND_CORE: (img(BEHIND, 0), img(BEHIND, 1), mate),
        IMG_BEHIND_CORE_Y: (img(BEHIND, 2), img(BEHIND, 3), mate),
        IMG_AHEAD_CORE: (img(AHEAD, 0), img(AHEAD, 1), mate),
        IMG_AHEAD_CORE_Y: (img(AHEAD, 2), img(AHEAD, 3), mate),
        IMG_FAR_CORE: (img(cross_group, 0), img(FAR, 1), cross),
        IMG_FAR_Y: (img(far_group, 2), img(FAR, 2), far_to),
        IMG_FAR_CORE_Y: (img(FAR, 2), img(FAR, 3), mate),
        TXT_Y: (txt(0, 0), txt(1, 0), y_far),
    }
    for h in range(2):
        gather[TXT_RIGHT + h] = (txt(h, 0), txt(h, 3), right)
        gather[TXT_LEFT + h] = (txt(h, 0), txt(h, 1), left)
        gather[TXT_RIGHT2 + h] = (
            txts.at[h, pl.ds(3 * rows, half)],
            txts.at[h, upper_part],
            right,
        )
        gather[TXT_LEFT2 + h] = (
            txts.at[h, pl.ds(rows + half, half)],
            txts.at[h, lower_part],
            left,
        )
    home = {
        IMG_FAR_Y: far_home,
        IMG_UP: down,
        IMG_DOWN: up,
        IMG_UP_Y: down,
        IMG_DOWN_Y: up,
    }
    for h in range(2):
        home[TXT_RIGHT + h] = home[TXT_RIGHT2 + h] = left
        home[TXT_LEFT + h] = home[TXT_LEFT2 + h] = right

    def back_buffers(index):
        if index < TXT_Y:
            return image_out.at[index], image_in.at[index]
        if index >= TXT_RIGHT2:
            return text_out.at[index - TXT_Y, pl.ds(0, half)], text_in.at[index - TXT_Y, pl.ds(0, half)]
        return text_out.at[index - TXT_Y], text_in.at[index - TXT_Y]

    def start(*indices):
        for index in indices:
            message(index, *gather[index]).start()

    def arrived(*indices):
        for index in indices:
            message(index, *gather[index]).wait_recv()

    def back_message(index):
        out, into = back_buffers(index)
        return message(BACK + index, out, into, home.get(index, gather[index][2]))

    def send_home(index, total, at):
        out, _ = back_buffers(index)
        out[...] = total[at].astype(BF16)
        back_message(index).start()

    def add_home(index, total, at):
        back_message(index).wait_recv()
        _, into = back_buffers(index)
        total[at] += into[...].astype(F32)

    scale = scale_ref[0]
    offset = offset_ref[0]
    unit_image, inv_image = unit_rows(image_ref[...])
    imgs[OWN, slot(0)] = unit_image.astype(BF16)
    unit_text, inv_text = unit_rows(text_ref[...])
    txts[0, slot(0)] = unit_text.astype(BF16)

    pl.semaphore_wait(barrier, 8)
    start(TXT_Y, IMG_Y, TXT_RIGHT, TXT_LEFT, IMG_UP, IMG_DOWN, IMG_CORE)
    image_sum[...] = jnp.zeros_like(image_sum)
    text_sum[...] = jnp.zeros_like(text_sum)
    imgs[FAR, slot(0)] = jnp.zeros((rows, width), BF16)
    arrived(IMG_Y)
    start(IMG_UP_Y, IMG_DOWN_Y, IMG_CORE_Y)
    arrived(TXT_Y)
    start(TXT_RIGHT + 1, TXT_LEFT + 1)
    arrived(IMG_UP, IMG_DOWN)
    start(IMG_FAR_CORE, IMG_BEHIND_CORE, IMG_AHEAD_CORE)
    arrived(TXT_RIGHT, TXT_LEFT)
    start(TXT_RIGHT2, TXT_LEFT2)
    arrived(IMG_UP_Y, IMG_DOWN_Y)
    start(IMG_FAR_Y, IMG_BEHIND_CORE_Y, IMG_AHEAD_CORE_Y)
    arrived(TXT_RIGHT + 1, TXT_LEFT + 1)
    start(TXT_RIGHT2 + 1, TXT_LEFT2 + 1)
    arrived(IMG_CORE, IMG_CORE_Y, TXT_RIGHT2, TXT_LEFT2)

    def coefficients(images, texts, target=None):
        logits = (
            lax.dot_general(images, texts, (((1,), (1,)), ((), ())), preferred_element_type=F32) * scale + offset
        )
        chance = 1.0 / (1.0 + jnp.exp(-logits))
        if target is not None:
            chance = chance - target
        return (scale * chance).astype(BF16)

    def tile(step, carry):
        h = step // 4
        turn = step % 4
        g = jnp.where(h == 0, turn, jnp.where(turn == 0, FAR, jnp.where(turn == 3, OWN, turn)))

        @pl.when(step == 1)
        def _():
            arrived(IMG_BEHIND_CORE, IMG_BEHIND_CORE_Y)

        @pl.when(step == 2)
        def _():
            arrived(IMG_AHEAD_CORE, IMG_AHEAD_CORE_Y)
            arrived(IMG_FAR_Y)
            start(IMG_FAR_CORE_Y)

        @pl.when(step == 3)
        def _():
            arrived(IMG_FAR_CORE, IMG_FAR_CORE_Y)

        @pl.when(step == 4)
        def _():
            arrived(TXT_RIGHT2 + 1, TXT_LEFT2 + 1)

        coeff = coefficients(imgs[g], txts[h])
        coeff_buf[...] = coeff
        coeff_t_buf[...] = coeff.T

        @pl.when(step == 0)
        def _():
            row = lax.broadcasted_iota(jnp.int32, (rows, rows), 0)
            column = lax.broadcasted_iota(jnp.int32, (rows, rows), 1)
            target = jnp.where(row == column, 1.0, 0.0).astype(F32)
            own = coefficients(imgs[OWN, slot(0)], txts[0, slot(0)], target)
            coeff_buf[:rows, :rows] = own
            coeff_t_buf[:rows, :rows] = own.T

        image_sum[g] += jnp.dot(coeff_buf[...], txts[h], preferred_element_type=F32)
        text_sum[h] += jnp.dot(coeff_t_buf[...], imgs[g], preferred_element_type=F32)
        return carry

    lax.fori_loop(0, 8, tile, 0)

    def text_part(h, k, begin=0, count=None):
        return (h, pl.ds(k * rows + begin, rows if count is None else count))

    for h in (1, 0):
        send_home(TXT_RIGHT2 + h, text_sum, text_part(h, 2, 0, half))
        send_home(TXT_LEFT2 + h, text_sum, text_part(h, 2, half, half))
    send_home(IMG_FAR_CORE_Y, image_sum, (FAR, slot(3)))
    send_home(IMG_FAR_CORE, image_sum, (FAR, slot(1)))
    send_home(IMG_BEHIND_CORE, image_sum, (BEHIND, slot(1)))
    send_home(IMG_BEHIND_CORE_Y, image_sum, (BEHIND, slot(3)))
    send_home(IMG_AHEAD_CORE, image_sum, (AHEAD, slot(1)))
    send_home(IMG_AHEAD_CORE_Y, image_sum, (AHEAD, slot(3)))
    send_home(IMG_CORE, image_sum, (OWN, slot(1)))
    send_home(IMG_CORE_Y, image_sum, (OWN, slot(3)))
    add_home(IMG_FAR_CORE_Y, image_sum, (FAR, slot(2)))
    send_home(IMG_FAR_Y, image_sum, (FAR, slot(2)))
    for h in (1, 0):
        add_home(TXT_RIGHT2 + h, text_sum, text_part(h, 3, 0, half))
        send_home(TXT_RIGHT + h, text_sum, text_part(h, 3))
        add_home(TXT_LEFT2 + h, text_sum, text_part(h, 1, half, half))
        send_home(TXT_LEFT + h, text_sum, text_part(h, 1))
    add_home(IMG_BEHIND_CORE, image_sum, (BEHIND, slot(0)))
    add_home(IMG_AHEAD_CORE, image_sum, (AHEAD, slot(0)))
    add_home(IMG_FAR_CORE, image_sum, (cross_group, slot(0)))
    send_home(IMG_UP, image_sum, (BEHIND, slot(0)))
    send_home(IMG_DOWN, image_sum, (AHEAD, slot(0)))
    add_home(IMG_BEHIND_CORE_Y, image_sum, (BEHIND, slot(2)))
    add_home(IMG_AHEAD_CORE_Y, image_sum, (AHEAD, slot(2)))
    add_home(IMG_FAR_Y, image_sum, (far_group, slot(2)))
    send_home(IMG_UP_Y, image_sum, (BEHIND, slot(2)))
    send_home(IMG_DOWN_Y, image_sum, (AHEAD, slot(2)))
    add_home(TXT_RIGHT + 1, text_sum, text_part(1, 0))
    add_home(TXT_LEFT + 1, text_sum, text_part(1, 0))
    send_home(TXT_Y, text_sum, text_part(1, 0))
    add_home(IMG_CORE_Y, image_sum, (OWN, slot(2)))
    add_home(IMG_UP_Y, image_sum, (OWN, slot(2)))
    add_home(IMG_DOWN_Y, image_sum, (OWN, slot(2)))
    send_home(IMG_Y, image_sum, (OWN, slot(2)))
    add_home(IMG_CORE, image_sum, (OWN, slot(0)))
    add_home(IMG_UP, image_sum, (OWN, slot(0)))
    add_home(IMG_DOWN, image_sum, (OWN, slot(0)))
    add_home(TXT_RIGHT, text_sum, text_part(0, 0))
    add_home(TXT_LEFT, text_sum, text_part(0, 0))
    add_home(TXT_Y, text_sum, text_part(0, 0))
    add_home(IMG_Y, image_sum, (OWN, slot(0)))

    def projected(embed, direction):
        unit, inverse = unit_rows(embed)
        return (direction - unit * jnp.sum(unit * direction, axis=1, keepdims=True)) * inverse

    image_grad_ref[...] = projected(image_ref[...], image_sum[OWN, slot(0)])
    text_grad_ref[...] = projected(text_ref[...], text_sum[0, slot(0)])

    for index in gather:
        message(index, *gather[index]).wait_send()
        back_message(index).wait_send()


def per_device(picture, caption, inverse_softness, similarity_offset):
    rows, width = picture.shape
    scalar = pl.BlockSpec(memory_space=pltpu.SMEM)
    whole = pl.BlockSpec(memory_space=pltpu.VMEM)
    pairs = 15 * rows * 8 * rows
    return pl.pallas_call(
        kernel,
        out_shape=(
            jax.ShapeDtypeStruct((rows, width), F32),
            jax.ShapeDtypeStruct((rows, width), F32),
        ),
        in_specs=[scalar, scalar, whole, whole],
        out_specs=(whole, whole),
        scratch_shapes=[
            pltpu.VMEM((4, 4 * rows, width), BF16),
            pltpu.VMEM((2, 4 * rows, width), BF16),
            pltpu.VMEM((4, 4 * rows, width), F32),
            pltpu.VMEM((2, 4 * rows, width), F32),
            pltpu.VMEM((4 * rows, 4 * rows), BF16),
            pltpu.VMEM((4 * rows, 4 * rows), BF16),
            pltpu.VMEM((14, rows, width), BF16),
            pltpu.VMEM((14, rows, width), BF16),
            pltpu.VMEM((9, rows, width), BF16),
            pltpu.VMEM((9, rows, width), BF16),
            pltpu.SemaphoreType.DMA((2 * BACK,)),
            pltpu.SemaphoreType.DMA((2 * BACK,)),
        ],
        compiler_params=pltpu.CompilerParams(
            collective_id=0, has_side_effects=True, vmem_limit_bytes=56 * 2**20
        ),
        cost_estimate=pl.CostEstimate(
            flops=6 * pairs * width, bytes_accessed=16 * rows * width, transcendentals=2 * pairs
        ),
    )(inverse_softness, similarity_offset, picture, caption)


def solution(mesh):
    spec = P(("blk", "group"), None)
    return jax.shard_map(
        per_device,
        mesh=mesh,
        in_specs=(spec, spec, P(), P()),
        out_specs=(spec, spec),
        check_vma=False,
    )
```

```python
import functools

import jax
import jax.numpy as jnp
from jax import lax
from jax.experimental import pallas as pl
from jax.experimental.pallas import tpu as pltpu
from jax.sharding import PartitionSpec as P

EPS = 1e-06
F32 = jnp.float32
BF16 = jnp.bfloat16

OWN, FIRST, SECOND, FAR = range(4)
MESSAGES = 23

OPENING = (
    ("+TYa", "+TR0a", "+TL0b", "+IYa", "+GUa", "+HUa", "+TR0b", "+TL0a", "+TYb", "+IYb", "+GUb", "+HUb", "+IC"),
)
BEFORE = {
    0: (
        ("-IYa", "+GYa", "+HYa", "+JYa", "-TR0a", "+HR0a", "-TL0b", "+HL0b", "-GUa", "+F1a", "-HUa", "+MCa", "+PCa"),
        ("-IYb", "+GYb", "+HYb", "+JYb", "-TYa", "+TR1a", "+TL1a", "-GUb", "+F1b", "-HUb", "+MCb", "+PCb"),
        ("-TYb", "+TL1b", "+TR1b", "-GYa", "+F2a", "-HYa", "+KYa", "+LYa"),
        ("-IC", "-JY", "-TR0b", "-TL0a", "-HR0a", "-HL0b"),
    ),
    1: (("-TR1a", "+HR1a", "-TL1b", "+HL1b", "-MC", "-PC"),),
    2: (("-GYb", "+F2b", "-HYb", "+KYb", "+LYb", "-F2a", "+F3a", "-KY", "-LY"),),
    3: (("-F2b", "+F3b", "-F1", "-F3"),),
    4: (("<HR0a", "<HL0b", "<TR0b", "<TL0a", "-TR1b", "-TL1a", "-HR1a", "-HL1b"),),
    5: (("<F3a", "<F3b", "<F1a", "<F1b"),),
    6: (("<LYa", "<KYa", "<LYb", "<KYb", ">HR0a", "<TR0a", ">HL0b", "<TL0b"),),
    7: (("<PCa", "<MCa", "<PCb", "<MCb"),),
}
WITHIN = {
    5: ((">F3a", "<F2a", ">F3b", "<F2b"),),
    6: ((">LYa", "<HYa", ">LYb", "<HYb"),),
    7: ((">MCa", ">PCa", "<HUa", ">MCb", ">PCb", "<HUb", ">KY"),),
}
CLOSING = (
    ("<HR1a", "<HL1b", "<TR1b", "<TL1a", "<JY", "<IC", ">F2a", "<GYa", ">F2b", "<GYb", ">F1a", "<GUa", ">F1b", "<GUb"),
    (">HR1a", "<TR1a", ">HL1b", "<TL1b", ">JY", ">HY", ">TR0", ">TL0", ">IC", ">HU"),
    (">TR1b", ">TL1b", "<TYb", ">GYa", "<IYa", ">TR1a", ">TL1a", "<TYa", ">GYb", "<IYb", ">GU"),
    (">IYa", ">IYb"),
)
FINISH = ((">TYb", ">TYa"),)


def unit_rows(embed):
    inverse = lax.rsqrt(jnp.sum(embed * embed, axis=1, keepdims=True) + EPS)
    return embed * inverse, inverse


def kernel(
    scale_ref,
    offset_ref,
    image_ref,
    text_ref,
    image_grad_ref,
    text_grad_ref,
    imgs,
    txts,
    image_sum,
    text_sum,
    coeff_buf,
    coeff_t_buf,
    sums_out,
    sums_in,
    send_sem,
    recv_sem,
):
    rows, width = image_ref.shape
    half = rows // 2
    n_blk = lax.axis_size("blk")
    blk = lax.axis_index("blk")
    group = lax.axis_index("group")
    core = blk % 2
    y = (blk // 2) % 2

    def device(dz=0, flip=0, dx=0, flip_y=0):
        plane = (blk // 4 + dz + n_blk // 4) % (n_blk // 4)
        within = blk % 4
        if flip % 2:
            within = within + 1 - 2 * core
        if flip // 2:
            within = within + 2 - 4 * y
        x = (group % 4 + dx + 4) % 4
        upper = group // 4
        if flip_y:
            upper = 1 - upper
        return (plane * 4 + within, upper * 4 + x)

    mate, y_near, y_far = device(flip=1), device(flip=2), device(flip_y=1)
    right, left = device(dx=1), device(dx=-1)
    cross, cross_back = device(dz=2 * core - 1, flip=1), device(dz=1 - 2 * core)
    core_on = device(dz=2 * core - 1)
    y_on, y_back = device(dz=1 - 2 * y), device(dz=2 * y - 1)

    barrier = pltpu.get_barrier_semaphore()
    for partner in (mate, y_near, core_on, cross_back, cross, right, left, y_far):
        pl.semaphore_signal(barrier, inc=1, device_id=partner, device_id_type=pl.DeviceIdType.MESH)

    def img(g, k):
        return imgs, image_sum, g, k * rows

    def txt(h, k):
        return txts, text_sum, h, k * rows

    def pair(g, which, k):
        return imgs, image_sum, g, pl.multiple_of(which * 2 * rows, rows) + k * rows

    routes = {
        "IY": (img(OWN, 0), img(OWN, 2), y_near, y_near),
        "IC": (img(OWN, 0), img(OWN, 1), mate, mate),
        "JY": (img(OWN, 2), img(OWN, 3), mate, mate),
        "GU": (img(OWN, 0), pair(FIRST, 1 - core, 0), core_on, cross_back),
        "HU": (img(OWN, 0), pair(FIRST, core, 0), cross_back, core_on),
        "GY": (img(OWN, 2), pair(SECOND, y, 0), y_on, y_back),
        "HY": (img(OWN, 2), pair(SECOND, 1 - y, 0), y_back, y_on),
        "MC": (img(FIRST, 0), img(FIRST, 1), mate, mate),
        "PC": (img(FIRST, 2), img(FIRST, 3), mate, mate),
        "KY": (pair(SECOND, y, 0), pair(SECOND, y, 1), mate, mate),
        "LY": (pair(SECOND, 1 - y, 0), pair(SECOND, 1 - y, 1), mate, mate),
        "F1": (pair(FIRST, 1 - core, 0), img(FAR, 1), cross, cross),
        "F2": (pair(SECOND, y, 0), img(FAR, 2), y_on, y_back),
        "F3": (img(FAR, 2), img(FAR, 3), mate, mate),
        "TY": (txt(0, 0), txt(1, 0), y_far, y_far),
    }
    for h in range(2):
        routes[f"TR{h}"] = (txt(h, 0), txt(h, 3), right, left)
        routes[f"TL{h}"] = (txt(h, 0), txt(h, 1), left, right)
        routes[f"HR{h}"] = (txt(h, 3), txt(h, 2), right, left)
        routes[f"HL{h}"] = (txt(h, 1), txt(h, 2), left, right)
    names = list(routes)
    sent = []

    def copy(index, source, target, to):
        return pltpu.make_async_remote_copy(
            src_ref=source,
            dst_ref=target,
            send_sem=send_sem.at[index],
            recv_sem=recv_sem.at[index],
            device_id=to,
            device_id_type=pl.DeviceIdType.MESH,
        )

    def gather(name, part):
        (source, _, g, row), (target, _, g_to, row_to), to, _ = routes[name]
        return copy(
            2 * names.index(name) + part,
            source.at[g, pl.ds(row + part * half, half)],
            target.at[g_to, pl.ds(row_to + part * half, half)],
            to,
        )

    def back(name, part):
        index = 2 * names.index(name) + part
        return copy(2 * len(names) + index, sums_out.at[index], sums_in.at[index], routes[name][3])

    def act(event):
        parts = (0, 1)
        kind, name = event[0], event[1:]
        if name[-1] in "ab":
            parts, name = ("ab".index(name[-1]),), name[:-1]
        for part in parts:
            index = 2 * names.index(name) + part
            (_, into, g_into, row_into), (_, total, g, row), _, _ = routes[name]
            if kind == "+":
                gather(name, part).start()
                sent.append((gather, name, part))
            elif kind == "-":
                gather(name, part).wait_recv()
            elif kind == "<":
                sums_out[index] = total[g, pl.ds(row + part * half, half)].astype(BF16)
                back(name, part).start()
                sent.append((back, name, part))
            else:
                back(name, part).wait_recv()
                into[g_into, pl.ds(row_into + part * half, half)] += sums_in[index].astype(F32)

    def act_all(events):
        for line in events:
            for event in line:
                act(event)

    scale = scale_ref[0]
    offset = offset_ref[0]
    unit_image, inv_image = unit_rows(image_ref[...])
    imgs[OWN, :rows] = unit_image.astype(BF16)
    unit_text, inv_text = unit_rows(text_ref[...])
    txts[0, :rows] = unit_text.astype(BF16)

    pl.semaphore_wait(barrier, 8)
    act_all(OPENING)
    image_sum[...] = jnp.zeros_like(image_sum)
    text_sum[...] = jnp.zeros_like(text_sum)
    imgs[FAR, :rows] = jnp.zeros((rows, width), BF16)

    def coefficients(images, texts, target=None):
        logits = (
            lax.dot_general(images, texts, (((1,), (1,)), ((), ())), preferred_element_type=F32) * scale + offset
        )
        chance = 1.0 / (1.0 + jnp.exp(-logits))
        if target is not None:
            chance = chance - target
        return (scale * chance).astype(BF16)

    def tile(step, carry):
        h = step // 4
        g = jnp.where(h == 0, step, 7 - step)
        for when, events in BEFORE.items():
            pl.when(step == when)(functools.partial(act_all, events))

        coeff = coefficients(imgs[g], txts[h])
        coeff_buf[...] = coeff
        coeff_t_buf[...] = coeff.T

        @pl.when(step == 0)
        def _():
            row = lax.broadcasted_iota(jnp.int32, (rows, rows), 0)
            column = lax.broadcasted_iota(jnp.int32, (rows, rows), 1)
            target = jnp.where(row == column, 1.0, 0.0).astype(F32)
            own = coefficients(imgs[OWN, :rows], txts[0, :rows], target)
            coeff_buf[:rows, :rows] = own
            coeff_t_buf[:rows, :rows] = own.T

        for when, events in WITHIN.items():
            pl.when(step == when)(functools.partial(act_all, events))

        image_sum[g] += jnp.dot(coeff_buf[...], txts[h], preferred_element_type=F32)
        text_sum[h] += jnp.dot(coeff_t_buf[...], imgs[g], preferred_element_type=F32)
        return carry

    lax.fori_loop(0, 8, tile, 0)
    act_all(CLOSING)

    def projected(embed, direction):
        unit, inverse = unit_rows(embed)
        return (direction - unit * jnp.sum(unit * direction, axis=1, keepdims=True)) * inverse

    image_grad_ref[...] = projected(image_ref[...], image_sum[OWN, :rows])
    act_all(FINISH)
    text_grad_ref[...] = projected(text_ref[...], text_sum[0, :rows])

    for kind, name, part in sent:
        kind(name, part).wait_send()


def per_device(picture, caption, inverse_softness, similarity_offset):
    rows, width = picture.shape
    scalar = pl.BlockSpec(memory_space=pltpu.SMEM)
    whole = pl.BlockSpec(memory_space=pltpu.VMEM)
    pairs = 15 * rows * 8 * rows
    return pl.pallas_call(
        kernel,
        out_shape=(
            jax.ShapeDtypeStruct((rows, width), F32),
            jax.ShapeDtypeStruct((rows, width), F32),
        ),
        in_specs=[scalar, scalar, whole, whole],
        out_specs=(whole, whole),
        scratch_shapes=[
            pltpu.VMEM((4, 4 * rows, width), BF16),
            pltpu.VMEM((2, 4 * rows, width), BF16),
            pltpu.VMEM((4, 4 * rows, width), F32),
            pltpu.VMEM((2, 4 * rows, width), F32),
            pltpu.VMEM((4 * rows, 4 * rows), BF16),
            pltpu.VMEM((4 * rows, 4 * rows), BF16),
            pltpu.VMEM((2 * MESSAGES, rows // 2, width), BF16),
            pltpu.VMEM((2 * MESSAGES, rows // 2, width), BF16),
            pltpu.SemaphoreType.DMA((4 * MESSAGES,)),
            pltpu.SemaphoreType.DMA((4 * MESSAGES,)),
        ],
        compiler_params=pltpu.CompilerParams(
            collective_id=0, has_side_effects=True, vmem_limit_bytes=56 * 2**20
        ),
        cost_estimate=pl.CostEstimate(
            flops=6 * pairs * width, bytes_accessed=16 * rows * width, transcendentals=2 * pairs
        ),
    )(inverse_softness, similarity_offset, picture, caption)


def solution(mesh):
    spec = P(("blk", "group"), None)
    return jax.shard_map(
        per_device,
        mesh=mesh,
        in_specs=(spec, spec, P(), P()),
        out_specs=(spec, spec),
        check_vma=False,
    )
```

```python
import functools

import jax
import jax.numpy as jnp
from jax import lax
from jax.experimental import pallas as pl
from jax.experimental.pallas import tpu as pltpu
from jax.sharding import PartitionSpec as P

EPS = 1e-06
LOG2_E = 1.4426950408889634
F32 = jnp.float32
BF16 = jnp.bfloat16

UNITS = 8
MESSAGES = 24

OPENING = (
    ("+IYa", "+TYa", "+AUa", "+BUa", "+TR0a", "+TL0b", "+TYb", "+AUb", "+BUb", "+TR0b", "+TL0a", "+IC"),
)
ORDER = (
    (0, 0), (2, 0), (3, 0), (6, 0), (1, 0), (8, 0), (7, 0), (9, 0),
    (7, 1), (6, 1), (8, 1), (9, 1), (2, 1), (3, 1), (1, 1), (0, 1),
)
BEFORE = {
    0: (
        ("-IYa", "+GYa", "+ZYa", "+JYa", "-AUa", "-BUa", "+MCa", "+PCa", "-TR0a", "+HR0a", "-TL0b", "+HL0b"),
        ("-TYa", "+TR1a", "+TL1a", "-AUb", "-BUb", "+SYb", "+IYb", "+F1", "+MCb", "+PCb"),
        ("-TYb", "+TR1b", "+TL1b", "-IC", "-TR0b", "-TL0a", "-HR0a", "-HL0b"),
    ),
    1: (("-GYa", "+F2a", "+KYa", "-MC", "-PC"),),
    2: (("-TR1a", "+HR1a", "-TL1b", "+HL1b"),),
    3: (("-SYb", "+F2b", "+KYb", "-F1"),),
    4: (("-IYb", "+ZYb", "+JYb", "-JY"),),
    5: (("-ZYa", "+LYa", "-KY"),),
    6: (("-F2a", "+F3a", "-F2b", "+F3b", "-F3"),),
    7: (("-ZYb", "+LYb", "-LY"),),
    8: (("<HR0a", "<HL0b", "<TR0b", "<TL0a", "-TR1b", "-TL1a", "-HR1a", "-HL1b"),),
    9: (("<F3",),),
    10: ((">F3a", "<F2a", ">F3b", "<F2b", "<F1"),),
    11: (("<KY",),),
    12: (("<LY", ">KY", ">HR0a", "<TR0a", ">HL0b", "<TL0b"),),
    13: ((">LY", "<ZY"),),
    14: (("<MC", "<PC", ">F2a", "<GYa"),),
    15: ((">MC", ">PC", ">F2b", "<SYb"),),
}
CLOSING = (
    ("<HR1a", "<HL1b", "<TR1b", "<TL1a", "<JY", "<IC", ">F1", "<AU", "<BUa", ">SYb", "<BUb"),
    (">HR1a", "<TR1a", ">HL1b", "<TL1b", ">JY", ">ZY", "<IYb", ">GYa", "<IYa", ">TR0", ">TL0", ">IC"),
    (">TR1b", ">TL1b", "<TYb", ">TR1a", ">TL1a", "<TYa", ">AU", ">IYb", ">BU"),
)
FINISH = (("image", "b", ()), ("image", "a", (">IYa",)), ("text", "b", (">TYb",)), ("text", "a", (">TYa",)))


def unit_rows(embed):
    inverse = lax.rsqrt(jnp.sum(embed * embed, axis=1, keepdims=True) + EPS)
    return embed * inverse, inverse


def kernel(
    scale_ref,
    offset_ref,
    image_ref,
    text_ref,
    image_grad_ref,
    text_grad_ref,
    imgs,
    txts,
    image_sum,
    text_sum,
    coeff_buf,
    coeff_t_buf,
    sums_out,
    sums_in,
    send_sem,
    recv_sem,
):
    rows, width = image_ref.shape
    half = rows // 2
    n_blk = lax.axis_size("blk")
    blk = lax.axis_index("blk")
    group = lax.axis_index("group")
    core = blk % 2
    y = (blk // 2) % 2

    def device(dz=0, flip=0, dx=0, flip_y=0):
        plane = (blk // 4 + dz + n_blk // 4) % (n_blk // 4)
        within = blk % 4
        if flip % 2:
            within = within + 1 - 2 * core
        if flip // 2:
            within = within + 2 - 4 * y
        x = (group % 4 + dx + 4) % 4
        upper = group // 4
        if flip_y:
            upper = 1 - upper
        return (plane * 4 + within, upper * 4 + x)

    mate, y_near, y_far = device(flip=1), device(flip=2), device(flip_y=1)
    right, left = device(dx=1), device(dx=-1)
    cross = device(dz=2 * core - 1, flip=1)
    y_on, y_back = device(dz=1 - 2 * y), device(dz=2 * y - 1)

    barrier = pltpu.get_barrier_semaphore()
    for partner in (mate, y_near, y_on, y_back, cross, right, left, y_far):
        pl.semaphore_signal(barrier, inc=1, device_id=partner, device_id_type=pl.DeviceIdType.MESH)

    def img(unit, k=0):
        return imgs, image_sum, unit, k * rows

    def txt(h, k):
        return txts, text_sum, h, k * rows

    own, own_y, on, back_, on_y, back_y = img(0), img(1), img(2 + y), img(3 - y), img(4 + y), img(5 - y)

    routes = {
        "IY": (own, own_y, y_near, y_near),
        "IC": (own, img(0, 1), mate, mate),
        "JY": (own_y, img(1, 1), mate, mate),
        "AU": (own, on, y_on, y_back),
        "BU": (own, back_, y_back, y_on),
        "GY": (own_y, on_y, y_on, y_back),
        "SY": (back_, back_y, y_near, y_near, on_y),
        "ZY": (own_y, back_y, y_back, y_on),
        "MC": (img(2), img(2, 1), mate, mate),
        "PC": (img(3), img(3, 1), mate, mate),
        "KY": (on_y, img(4 + y, 1), mate, mate),
        "LY": (back_y, img(5 - y, 1), mate, mate),
        "F1": (img(3 - core), img(6), cross, cross),
        "F2": (on_y, img(7), y_on, y_back),
        "F3": (img(7), img(7, 1), mate, mate),
        "TY": (txt(0, 0), txt(1, 0), y_far, y_far),
    }
    for h in range(2):
        routes[f"TR{h}"] = (txt(h, 0), txt(h, 3), right, left)
        routes[f"TL{h}"] = (txt(h, 0), txt(h, 1), left, right)
        routes[f"HR{h}"] = (txt(h, 3), txt(h, 2), right, left)
        routes[f"HL{h}"] = (txt(h, 1), txt(h, 2), left, right)
    names = list(routes)
    joins = {
        "F2": ("F3",),
        "GY": ("KY", "F2"),
        "SY": ("KY", "F2"),
        "ZY": ("LY",),
        "IY": ("JY", "ZY", "GY"),
        "image": ("IC", "IY", "AU", "BU"),
        "TY": ("TR1", "TL1"),
        "text": ("TR0", "TL0", "TY"),
    }
    for h in range(2):
        joins[f"TR{h}"], joins[f"TL{h}"] = (f"HR{h}",), (f"HL{h}",)
    in_place = ("MC", "PC", "F1", "SY")
    sent, added = [], set()

    def copy(index, source, target, to):
        return pltpu.make_async_remote_copy(
            src_ref=source,
            dst_ref=target,
            send_sem=send_sem.at[index],
            recv_sem=recv_sem.at[index],
            device_id=to,
            device_id_type=pl.DeviceIdType.MESH,
        )

    def at(place, part):
        return place[2], pl.ds(place[3] + part * half, half)

    def gather(name, part):
        source, target, to = routes[name][:3]
        return copy(
            2 * names.index(name) + part, source[0].at[at(source, part)], target[0].at[at(target, part)], to
        )

    def back(name, part):
        index = 2 * names.index(name) + part
        return copy(2 * len(names) + index, sums_out.at[index], sums_in.at[index], routes[name][3])

    def total(name, place, part):
        value = place[1][at(place, part)]
        for other in joins.get(name, ()):
            if (other, part) in added:
                value = value + sums_in[2 * names.index(other) + part].astype(F32)
        return value

    def act(event):
        parts = (0, 1)
        kind, name = event[0], event[1:]
        if name[-1] in "ab":
            parts, name = ("ab".index(name[-1]),), name[:-1]
        for part in parts:
            index = 2 * names.index(name) + part
            if kind == "+":
                gather(name, part).start()
                sent.append((gather, name, part))
            elif kind == "-":
                gather(name, part).wait_recv()
            elif kind == "<":
                sums_out[index] = total(name, (routes[name] + routes[name][1:2])[4], part).astype(BF16)
                back(name, part).start()
                sent.append((back, name, part))
            else:
                back(name, part).wait_recv()
                if name in in_place:
                    place = routes[name][0]
                    place[1][at(place, part)] += sums_in[index].astype(F32)
                else:
                    added.add((name, part))

    def act_all(events):
        for line in events:
            for event in line:
                act(event)

    scale = scale_ref[0]
    offset = offset_ref[0]
    unit_image, inv_image = unit_rows(image_ref[...])
    imgs[0, :rows] = unit_image.astype(BF16)
    unit_text, inv_text = unit_rows(text_ref[...])
    txts[0, :rows] = unit_text.astype(BF16)

    pl.semaphore_wait(barrier, 8)
    act_all(OPENING)
    image_sum[...] = jnp.zeros_like(image_sum)
    text_sum[...] = jnp.zeros_like(text_sum)
    imgs[6, rows:] = jnp.zeros((rows, width), BF16)

    row = lax.broadcasted_iota(jnp.int32, (rows, rows), 0)
    column = lax.broadcasted_iota(jnp.int32, (rows, rows), 1)
    diagonal = jnp.where(row == column, 1.0, 0.0).astype(F32)
    slope, level = scale * -LOG2_E, offset * -LOG2_E

    def pick(step, values):
        picked = values[0]
        for i, value in enumerate(values[1:]):
            picked = jnp.where(step > i, value, picked)
        return picked

    def tile(step, carry):
        unit = pick(step, [{8: 4 + y, 9: 5 - y}.get(u, u) for u, _ in ORDER])
        h = pick(step, [h for _, h in ORDER])
        for when, events in BEFORE.items():
            pl.when(step == when)(functools.partial(act_all, events))

        logits = lax.dot_general(
            imgs[unit], txts[h], (((1,), (1,)), ((), ())), preferred_element_type=F32
        )
        chance = 1.0 / (1.0 + jnp.exp2(logits * slope + level))
        corner = chance[:rows, :rows] - jnp.where(step == 0, 1.0, 0.0) * diagonal
        edge = jnp.concatenate([corner, chance[rows:, :rows]], axis=0)
        coeff = (scale * jnp.concatenate([edge, chance[:, rows:]], axis=1)).astype(BF16)
        coeff_buf[...] = coeff
        coeff_t_buf[...] = coeff.T
        image_sum[unit] += jnp.dot(coeff_buf[...], txts[h], preferred_element_type=F32)
        text_sum[h] += jnp.dot(coeff_t_buf[...], imgs[unit], preferred_element_type=F32)
        return carry

    lax.fori_loop(0, len(ORDER), tile, 0)
    act_all(CLOSING)

    for side, which, events in FINISH:
        act_all((events,))
        part = "ab".index(which)
        here = pl.ds(part * half, half)
        embed_ref, place, out_ref = {
            "image": (image_ref, own, image_grad_ref),
            "text": (text_ref, txt(0, 0), text_grad_ref),
        }[side]
        unit_part, inverse = unit_rows(embed_ref[here])
        direction = total(side, place, part)
        along = jnp.sum(unit_part * direction, axis=1, keepdims=True)
        out_ref[here] = (direction - unit_part * along) * inverse

    for kind, name, part in sent:
        kind(name, part).wait_send()


def per_device(picture, caption, inverse_softness, similarity_offset):
    rows, width = picture.shape
    scalar = pl.BlockSpec(memory_space=pltpu.SMEM)
    whole = pl.BlockSpec(memory_space=pltpu.VMEM)
    pairs = 15 * rows * 8 * rows
    return pl.pallas_call(
        kernel,
        out_shape=(
            jax.ShapeDtypeStruct((rows, width), F32),
            jax.ShapeDtypeStruct((rows, width), F32),
        ),
        in_specs=[scalar, scalar, whole, whole],
        out_specs=(whole, whole),
        scratch_shapes=[
            pltpu.VMEM((UNITS, 2 * rows, width), BF16),
            pltpu.VMEM((2, 4 * rows, width), BF16),
            pltpu.VMEM((UNITS, 2 * rows, width), F32),
            pltpu.VMEM((2, 4 * rows, width), F32),
            pltpu.VMEM((2 * rows, 4 * rows), BF16),
            pltpu.VMEM((4 * rows, 2 * rows), BF16),
            pltpu.VMEM((2 * MESSAGES, rows // 2, width), BF16),
            pltpu.VMEM((2 * MESSAGES, rows // 2, width), BF16),
            pltpu.SemaphoreType.DMA((4 * MESSAGES,)),
            pltpu.SemaphoreType.DMA((4 * MESSAGES,)),
        ],
        compiler_params=pltpu.CompilerParams(
            collective_id=0, has_side_effects=True, vmem_limit_bytes=56 * 2**20
        ),
        cost_estimate=pl.CostEstimate(
            flops=6 * pairs * width, bytes_accessed=16 * rows * width, transcendentals=2 * pairs
        ),
    )(inverse_softness, similarity_offset, picture, caption)


def solution(mesh):
    spec = P(("blk", "group"), None)
    return jax.shard_map(
        per_device,
        mesh=mesh,
        in_specs=(spec, spec, P(), P()),
        out_specs=(spec, spec),
        check_vma=False,
    )
```

```python
import functools

import jax
import jax.numpy as jnp
from jax import lax
from jax.experimental import pallas as pl
from jax.experimental.pallas import tpu as pltpu
from jax.sharding import PartitionSpec as P

EPS = 1e-06
LOG2_E = 1.4426950408889634
F32 = jnp.float32
BF16 = jnp.bfloat16

UNITS = 8
MESSAGES = 24

OPENING = (
    ("+TYa", "+IYa", "+AUa", "+BUa", "+TR0a", "+TL0b", "+TYb", "+IYb", "+AUb", "+BUb", "+TR0b", "+TL0a", "+IC"),
)
ORDER = (
    (0, 0), (2, 0), (3, 0), (1, 0), (6, 0), (8, 0), (1, 1), (6, 1),
    (9, 0), (7, 0), (7, 1), (9, 1), (8, 1), (2, 1), (3, 1), (0, 1),
)
BEFORE = {
    0: (
        ("-TR0a", "+HR0a", "-TL0b", "+HL0b", "-TYa", "+TR1a", "+TL1a", "-AUa", "-BUa", "+MCa", "+PCa"),
        ("-IYa", "+GYa", "+ZYa", "+JYa", "-AUb", "-BUb", "+SYb", "+F1", "+MCb", "+PCb"),
        ("-TYb", "+TR1b", "+TL1b", "-IC", "-TR0b", "-TL0a", "-HR0a", "-HL0b"),
    ),
    1: (("-GYa", "+F2a", "+KYa", "-MC", "-PC"),),
    2: (("-IYb", "+ZYb", "+JYb"),),
    3: (("-JY", "-TR1a", "+HR1a", "-TL1b", "+HL1b"),),
    4: (("-F1", "-SYb", "+F2b", "+KYb"),),
    5: (("-KY", "-ZYa", "+LYa"),),
    6: (("-ZYb", "+LYb", "-TR1b", "-TL1a", "-HR1a", "-HL1b"),),
    7: (("-F2a", "+F3a", "<JY"),),
    8: (("-LY", "-F2b", "+F3b", "<F1"),),
    9: (("-F3",),),
    10: (("<HR0a", "<HL0b", "<TR0b", "<TL0a"),),
    11: (("<F3",),),
    12: (("<LY", ">F3a", "<F2a", ">F3b", "<F2b"),),
    13: ((">LY", "<ZY", "<KY"),),
    14: ((">HR0a", "<TR0a", ">HL0b", "<TL0b", ">KY", ">F1", ">JY"),),
    15: (("<MC", "<PC"),),
}
CLOSING = (
    ("<HR1a", "<HL1b", "<TR1b", "<TL1a", ">F2a", "<GYa", "<IC", ">MC", ">PC", "<AU", "<BUa", ">F2b", "<SYb"),
    (">ZYb", "<IYb", ">HR1a", "<TR1a", ">HL1b", "<TL1b", ">ZYa", ">GYa", "<IYa", ">SYb", "<BUb"),
    (">TR1b", ">TL1b", "<TYb", ">TR1a", ">TL1a", "<TYa", ">TR0", ">TL0", ">IC", ">AU", ">BUa"),
)
FINISH = (
    ("image", "a", (">IYa",)),
    ("image", "b", (">IYb", ">BUb")),
    ("text", "b", (">TYb",)),
    ("text", "a", (">TYa",)),
)


def unit_rows(embed):
    inverse = lax.rsqrt(jnp.sum(embed * embed, axis=1, keepdims=True) + EPS)
    return embed * inverse, inverse


def kernel(
    scale_ref,
    offset_ref,
    image_ref,
    text_ref,
    image_grad_ref,
    text_grad_ref,
    imgs,
    txts,
    image_sum,
    text_sum,
    coeff_buf,
    coeff_t_buf,
    sums_out,
    sums_in,
    send_sem,
    recv_sem,
):
    rows, width = image_ref.shape
    half = rows // 2
    n_blk = lax.axis_size("blk")
    blk = lax.axis_index("blk")
    group = lax.axis_index("group")
    core = blk % 2
    y = (blk // 2) % 2

    def device(dz=0, flip=0, dx=0, flip_y=0):
        plane = (blk // 4 + dz + n_blk // 4) % (n_blk // 4)
        within = blk % 4
        if flip % 2:
            within = within + 1 - 2 * core
        if flip // 2:
            within = within + 2 - 4 * y
        x = (group % 4 + dx + 4) % 4
        upper = group // 4
        if flip_y:
            upper = 1 - upper
        return (plane * 4 + within, upper * 4 + x)

    mate, y_near, y_far = device(flip=1), device(flip=2), device(flip_y=1)
    right, left = device(dx=1), device(dx=-1)
    cross = device(dz=2 * core - 1, flip=1)
    y_on, y_back = device(dz=1 - 2 * y), device(dz=2 * y - 1)

    barrier = pltpu.get_barrier_semaphore()
    for partner in (mate, y_near, y_on, y_back, cross, right, left, y_far):
        pl.semaphore_signal(barrier, inc=1, device_id=partner, device_id_type=pl.DeviceIdType.MESH)

    def img(unit, k=0):
        return imgs, image_sum, unit, k * rows

    def txt(h, k):
        return txts, text_sum, h, k * rows

    own, own_y, on, back_, on_y, back_y = img(0), img(1), img(2 + y), img(3 - y), img(4 + y), img(5 - y)

    routes = {
        "IY": (own, own_y, y_near, y_near),
        "IC": (own, img(0, 1), mate, mate),
        "JY": (own_y, img(1, 1), mate, mate),
        "AU": (own, on, y_on, y_back),
        "BU": (own, back_, y_back, y_on),
        "GY": (own_y, on_y, y_on, y_back),
        "SY": (back_, back_y, y_near, y_near, on_y),
        "ZY": (own_y, back_y, y_back, y_on),
        "MC": (img(2), img(2, 1), mate, mate),
        "PC": (img(3), img(3, 1), mate, mate),
        "KY": (on_y, img(4 + y, 1), mate, mate),
        "LY": (back_y, img(5 - y, 1), mate, mate),
        "F1": (img(3 - core), img(6), cross, cross),
        "F2": (on_y, img(7), y_on, y_back),
        "F3": (img(7), img(7, 1), mate, mate),
        "TY": (txt(0, 0), txt(1, 0), y_far, y_far),
    }
    for h in range(2):
        routes[f"TR{h}"] = (txt(h, 0), txt(h, 3), right, left)
        routes[f"TL{h}"] = (txt(h, 0), txt(h, 1), left, right)
        routes[f"HR{h}"] = (txt(h, 3), txt(h, 2), right, left)
        routes[f"HL{h}"] = (txt(h, 1), txt(h, 2), left, right)
    names = list(routes)
    joins = {
        "F2": ("F3",),
        "GY": ("KY", "F2"),
        "SY": ("KY", "F2"),
        "ZY": ("LY",),
        "IY": ("JY", "ZY", "GY"),
        "image": ("IC", "IY", "AU", "BU"),
        "TY": ("TR1", "TL1"),
        "text": ("TR0", "TL0", "TY"),
    }
    for h in range(2):
        joins[f"TR{h}"], joins[f"TL{h}"] = (f"HR{h}",), (f"HL{h}",)
    in_place = ("MC", "PC", "F1", "SY")
    sent, added = [], set()

    def copy(index, source, target, to):
        return pltpu.make_async_remote_copy(
            src_ref=source,
            dst_ref=target,
            send_sem=send_sem.at[index],
            recv_sem=recv_sem.at[index],
            device_id=to,
            device_id_type=pl.DeviceIdType.MESH,
        )

    def at(place, part):
        return place[2], pl.ds(place[3] + part * half, half)

    def gather(name, part):
        source, target, to = routes[name][:3]
        return copy(
            2 * names.index(name) + part, source[0].at[at(source, part)], target[0].at[at(target, part)], to
        )

    def back(name, part):
        index = 2 * names.index(name) + part
        return copy(2 * len(names) + index, sums_out.at[index], sums_in.at[index], routes[name][3])

    def total(name, place, part):
        value = place[1][at(place, part)]
        for other in joins.get(name, ()):
            if (other, part) in added:
                value = value + sums_in[2 * names.index(other) + part].astype(F32)
        return value

    def act(event):
        parts = (0, 1)
        kind, name = event[0], event[1:]
        if name[-1] in "ab":
            parts, name = ("ab".index(name[-1]),), name[:-1]
        for part in parts:
            index = 2 * names.index(name) + part
            if kind == "+":
                gather(name, part).start()
                sent.append((gather, name, part))
            elif kind == "-":
                gather(name, part).wait_recv()
            elif kind == "<":
                sums_out[index] = total(name, (routes[name] + routes[name][1:2])[4], part).astype(BF16)
                back(name, part).start()
                sent.append((back, name, part))
            else:
                back(name, part).wait_recv()
                if name in in_place:
                    place = routes[name][0]
                    place[1][at(place, part)] += sums_in[index].astype(F32)
                else:
                    added.add((name, part))

    def act_all(events):
        for line in events:
            for event in line:
                act(event)

    scale = scale_ref[0]
    offset = offset_ref[0]
    unit_image, inv_image = unit_rows(image_ref[...])
    imgs[0, :rows] = unit_image.astype(BF16)
    unit_text, inv_text = unit_rows(text_ref[...])
    txts[0, :rows] = unit_text.astype(BF16)

    pl.semaphore_wait(barrier, 8)
    act_all(OPENING)
    image_sum[...] = jnp.zeros_like(image_sum)
    text_sum[...] = jnp.zeros_like(text_sum)
    imgs[6, rows:] = jnp.zeros((rows, width), BF16)

    row = lax.broadcasted_iota(jnp.int32, (rows, rows), 0)
    column = lax.broadcasted_iota(jnp.int32, (rows, rows), 1)
    diagonal = jnp.where(row == column, 1.0, 0.0).astype(F32)
    slope, level = scale * -LOG2_E, offset * -LOG2_E

    def pick(step, values):
        picked = values[0]
        for i, value in enumerate(values[1:]):
            picked = jnp.where(step > i, value, picked)
        return picked

    def tile(step, carry):
        unit = pick(step, [{8: 4 + y, 9: 5 - y}.get(u, u) for u, _ in ORDER])
        h = pick(step, [h for _, h in ORDER])
        for when, events in BEFORE.items():
            pl.when(step == when)(functools.partial(act_all, events))

        logits = lax.dot_general(
            imgs[unit], txts[h], (((1,), (1,)), ((), ())), preferred_element_type=F32
        )
        chance = 1.0 / (1.0 + jnp.exp2(logits * slope + level))
        corner = chance[:rows, :rows] - jnp.where(step == 0, 1.0, 0.0) * diagonal
        edge = jnp.concatenate([corner, chance[rows:, :rows]], axis=0)
        coeff = (scale * jnp.concatenate([edge, chance[:, rows:]], axis=1)).astype(BF16)
        coeff_buf[...] = coeff
        coeff_t_buf[...] = coeff.T
        image_sum[unit] += jnp.dot(coeff_buf[...], txts[h], preferred_element_type=F32)
        text_sum[h] += jnp.dot(coeff_t_buf[...], imgs[unit], preferred_element_type=F32)
        return carry

    lax.fori_loop(0, len(ORDER), tile, 0)
    act_all(CLOSING)

    for side, which, events in FINISH:
        act_all((events,))
        part = "ab".index(which)
        here = pl.ds(part * half, half)
        embed_ref, place, out_ref = {
            "image": (image_ref, own, image_grad_ref),
            "text": (text_ref, txt(0, 0), text_grad_ref),
        }[side]
        unit_part, inverse = unit_rows(embed_ref[here])
        direction = total(side, place, part)
        along = jnp.sum(unit_part * direction, axis=1, keepdims=True)
        out_ref[here] = (direction - unit_part * along) * inverse

    for kind, name, part in sent:
        kind(name, part).wait_send()


def per_device(picture, caption, inverse_softness, similarity_offset):
    rows, width = picture.shape
    scalar = pl.BlockSpec(memory_space=pltpu.SMEM)
    whole = pl.BlockSpec(memory_space=pltpu.VMEM)
    pairs = 15 * rows * 8 * rows
    return pl.pallas_call(
        kernel,
        out_shape=(
            jax.ShapeDtypeStruct((rows, width), F32),
            jax.ShapeDtypeStruct((rows, width), F32),
        ),
        in_specs=[scalar, scalar, whole, whole],
        out_specs=(whole, whole),
        scratch_shapes=[
            pltpu.VMEM((UNITS, 2 * rows, width), BF16),
            pltpu.VMEM((2, 4 * rows, width), BF16),
            pltpu.VMEM((UNITS, 2 * rows, width), F32),
            pltpu.VMEM((2, 4 * rows, width), F32),
            pltpu.VMEM((2 * rows, 4 * rows), BF16),
            pltpu.VMEM((4 * rows, 2 * rows), BF16),
            pltpu.VMEM((2 * MESSAGES, rows // 2, width), BF16),
            pltpu.VMEM((2 * MESSAGES, rows // 2, width), BF16),
            pltpu.SemaphoreType.DMA((4 * MESSAGES,)),
            pltpu.SemaphoreType.DMA((4 * MESSAGES,)),
        ],
        compiler_params=pltpu.CompilerParams(
            collective_id=0, has_side_effects=True, vmem_limit_bytes=56 * 2**20
        ),
        cost_estimate=pl.CostEstimate(
            flops=6 * pairs * width, bytes_accessed=16 * rows * width, transcendentals=2 * pairs
        ),
    )(inverse_softness, similarity_offset, picture, caption)


def solution(mesh):
    spec = P(("blk", "group"), None)
    return jax.shard_map(
        per_device,
        mesh=mesh,
        in_specs=(spec, spec, P(), P()),
        out_specs=(spec, spec),
        check_vma=False,
    )
```

```python
import functools

import jax
import jax.numpy as jnp
from jax import lax
from jax.experimental import pallas as pl
from jax.experimental.pallas import tpu as pltpu
from jax.sharding import PartitionSpec as P

EPS = 1e-06
LOG2_E = 1.4426950408889634
F32 = jnp.float32
BF16 = jnp.bfloat16

UNITS = 8
MESSAGES = 24

OPENING = (
    ("+TYa", "+IYa", "+AUa", "+BUa", "+TR0a", "+TL0b", "+TYb", "+AUb", "+BUb", "+TR0b",),
    ("+TL0a", "+IC",),
)
ORDER = (
    (0, 0), (2, 0), (3, 0), (1, 0), (6, 0), (8, 0), (1, 1), (6, 1),
    (9, 0), (7, 0), (7, 1), (9, 1), (8, 1), (2, 1), (3, 1), (0, 1),
)
BEFORE = {
    0: (
        ("-TR0a", "+HR0a", "-TL0b", "+HL0b", "-TYa", "+TR1a", "+TL1a", "-AUa", "-BUa", "+MCa",),
        ("+PCa", "-IYa", "+GYa", "+ZYa", "+JYa", "-AUb", "-BUb", "+SYb", "+IYb", "+F1",),
        ("+MCb", "+PCb", "-TYb", "+TR1b", "+TL1b", "-IC", "-TR0b", "-TL0a", "-HR0a", "-HL0b",),
    ),
    1: (
        ("-GYa", "+F2a", "+KYa", "-MC", "-PC",),
    ),
    2: (
        ("-IYb", "+ZYb", "+JYb",),
    ),
    3: (
        ("-JY", "-TR1a", "+HR1a", "-TL1b", "+HL1b",),
    ),
    4: (
        ("-F1", "-SYb", "+F2b", "+KYb",),
    ),
    5: (
        ("-KY", "-ZYa", "+LYa",),
    ),
    6: (
        ("-ZYb", "+LYb", "-TR1b", "-TL1a", "-HR1a", "-HL1b",),
    ),
    7: (
        ("-F2a", "+F3a", "<JY",),
    ),
    8: (
        ("-LY", "-F2b", "+F3b", "<F1",),
    ),
    9: (
        ("-F3",),
    ),
    10: (
        ("<HR0a", "<HL0b", "<TR0b", "<TL0a",),
    ),
    11: (
        ("<F3",),
    ),
    12: (
        ("<LY", ">F3a", "<F2a", ">F3b", "<F2b",),
    ),
    13: (
        (">LY", "<ZY", "<KY",),
    ),
    14: (
        (">HR0a", "<TR0a", ">HL0b", "<TL0b", ">KY", ">F1", ">JY",),
    ),
    15: (
        ("<MC", "<PC",),
    ),
}
CLOSING = (
    ("<HR1a", "<HL1b", "<TR1b", "<TL1a", ">F2a", "<GYa", "<IC", ">MC", ">PC", "<AU",),
    ("<BUa", ">F2b", "<SYb", ">ZYb", "<IYb", ">HR1a", "<TR1a", ">HL1b", "<TL1b", ">ZYa",),
    (">GYa", "<IYa", ">SYb", "<BUb", ">TR1b", ">TL1b", "<TYb", ">TR1a", ">TL1a", "<TYa",),
    (">TR0", ">TL0", ">IC", ">AU", ">BUa",),
)
FINISH = (
    ("image", "a", (">IYa",)),
    ("image", "b", (">IYb", ">BUb")),
    ("text", "b", (">TYb",)),
    ("text", "a", (">TYa",)),
)


def unit_rows(embed):
    inverse = lax.rsqrt(jnp.sum(embed * embed, axis=1, keepdims=True) + EPS)
    return embed * inverse, inverse


def kernel(
    scale_ref,
    offset_ref,
    image_ref,
    text_ref,
    grads_ref,
    imgs,
    txts,
    image_sum,
    text_sum,
    coeff_buf,
    coeff_t_buf,
    sums_out,
    sums_in,
    send_sem,
    recv_sem,
):
    rows, width = image_ref.shape
    half = rows // 2
    n_blk = lax.axis_size("blk")
    blk = lax.axis_index("blk")
    group = lax.axis_index("group")
    core = blk % 2
    y = (blk // 2) % 2

    def device(dz=0, flip=0, dx=0, flip_y=0):
        plane = (blk // 4 + dz + n_blk // 4) % (n_blk // 4)
        within = blk % 4
        if flip % 2:
            within = within + 1 - 2 * core
        if flip // 2:
            within = within + 2 - 4 * y
        x = (group % 4 + dx + 4) % 4
        upper = group // 4
        if flip_y:
            upper = 1 - upper
        return (plane * 4 + within, upper * 4 + x)

    mate, y_near, y_far = device(flip=1), device(flip=2), device(flip_y=1)
    right, left = device(dx=1), device(dx=-1)
    cross = device(dz=2 * core - 1, flip=1)
    y_on, y_back = device(dz=1 - 2 * y), device(dz=2 * y - 1)

    barrier = pltpu.get_barrier_semaphore()
    for partner in (mate, y_near, y_on, y_back, cross, right, left, y_far):
        pl.semaphore_signal(barrier, inc=1, device_id=partner, device_id_type=pl.DeviceIdType.MESH)

    def img(unit, k=0):
        return imgs, image_sum, unit, k * rows

    def txt(h, k):
        return txts, text_sum, h, k * rows

    own, own_y, on, back_, on_y, back_y = img(0), img(1), img(2 + y), img(3 - y), img(4 + y), img(5 - y)

    routes = {
        "IY": (own, own_y, y_near, y_near),
        "IC": (own, img(0, 1), mate, mate),
        "JY": (own_y, img(1, 1), mate, mate),
        "AU": (own, on, y_on, y_back),
        "BU": (own, back_, y_back, y_on),
        "GY": (own_y, on_y, y_on, y_back),
        "SY": (back_, back_y, y_near, y_near, on_y),
        "ZY": (own_y, back_y, y_back, y_on),
        "MC": (img(2), img(2, 1), mate, mate),
        "PC": (img(3), img(3, 1), mate, mate),
        "KY": (on_y, img(4 + y, 1), mate, mate),
        "LY": (back_y, img(5 - y, 1), mate, mate),
        "F1": (img(3 - core), img(6), cross, cross),
        "F2": (on_y, img(7), y_on, y_back),
        "F3": (img(7), img(7, 1), mate, mate),
        "TY": (txt(0, 0), txt(1, 0), y_far, y_far),
    }
    for h in range(2):
        routes[f"TR{h}"] = (txt(h, 0), txt(h, 3), right, left)
        routes[f"TL{h}"] = (txt(h, 0), txt(h, 1), left, right)
        routes[f"HR{h}"] = (txt(h, 3), txt(h, 2), right, left)
        routes[f"HL{h}"] = (txt(h, 1), txt(h, 2), left, right)
    names = list(routes)
    joins = {
        "F2": ("F3",),
        "GY": ("KY", "F2"),
        "SY": ("KY", "F2"),
        "ZY": ("LY",),
        "IY": ("JY", "ZY", "GY"),
        "image": ("IC", "IY", "AU", "BU"),
        "TY": ("TR1", "TL1"),
        "text": ("TR0", "TL0", "TY"),
    }
    for h in range(2):
        joins[f"TR{h}"], joins[f"TL{h}"] = (f"HR{h}",), (f"HL{h}",)
    in_place = ("MC", "PC", "F1", "SY")
    sent, added = [], set()

    def copy(index, source, target, to):
        return pltpu.make_async_remote_copy(
            src_ref=source,
            dst_ref=target,
            send_sem=send_sem.at[index],
            recv_sem=recv_sem.at[index],
            device_id=to,
            device_id_type=pl.DeviceIdType.MESH,
        )

    def at(place, part):
        return place[2], pl.ds(place[3] + part * half, half)

    def gather(name, part):
        source, target, to = routes[name][:3]
        return copy(
            2 * names.index(name) + part, source[0].at[at(source, part)], target[0].at[at(target, part)], to
        )

    def back(name, part):
        index = 2 * names.index(name) + part
        return copy(2 * len(names) + index, sums_out.at[index], sums_in.at[index], routes[name][3])

    def total(name, place, part):
        value = place[1][at(place, part)]
        for other in joins.get(name, ()):
            if (other, part) in added:
                value = value + sums_in[2 * names.index(other) + part].astype(F32)
        return value

    def act(event):
        parts = (0, 1)
        kind, name = event[0], event[1:]
        if name[-1] in "ab":
            parts, name = ("ab".index(name[-1]),), name[:-1]
        for part in parts:
            index = 2 * names.index(name) + part
            if kind == "+":
                gather(name, part).start()
                sent.append((gather, name, part))
            elif kind == "-":
                gather(name, part).wait_recv()
            elif kind == "<":
                sums_out[index] = total(name, (routes[name] + routes[name][1:2])[4], part).astype(BF16)
                back(name, part).start()
                sent.append((back, name, part))
            else:
                back(name, part).wait_recv()
                if name in in_place:
                    place = routes[name][0]
                    place[1][at(place, part)] += sums_in[index].astype(F32)
                else:
                    added.add((name, part))

    def act_all(events):
        for line in events:
            for event in line:
                act(event)

    scale = scale_ref[0]
    offset = offset_ref[0]
    unit_image, inv_image = unit_rows(image_ref[...])
    imgs[0, :rows] = unit_image.astype(BF16)
    unit_text, inv_text = unit_rows(text_ref[...])
    txts[0, :rows] = unit_text.astype(BF16)

    pl.semaphore_wait(barrier, 8)
    act_all(OPENING)
    image_sum[...] = jnp.zeros_like(image_sum)
    text_sum[...] = jnp.zeros_like(text_sum)
    imgs[6, rows:] = jnp.zeros((rows, width), BF16)

    row = lax.broadcasted_iota(jnp.int32, (rows, rows), 0)
    column = lax.broadcasted_iota(jnp.int32, (rows, rows), 1)
    diagonal = jnp.where(row == column, 1.0, 0.0).astype(F32)
    slope, level = scale * -LOG2_E, offset * -LOG2_E

    def pick(step, values):
        picked = values[0]
        for i, value in enumerate(values[1:]):
            picked = jnp.where(step > i, value, picked)
        return picked

    def tile(step, carry):
        unit = pick(step, [{8: 4 + y, 9: 5 - y}.get(u, u) for u, _ in ORDER])
        h = pick(step, [h for _, h in ORDER])
        for when, events in BEFORE.items():
            pl.when(step == when)(functools.partial(act_all, events))

        logits = lax.dot_general(
            imgs[unit], txts[h], (((1,), (1,)), ((), ())), preferred_element_type=F32
        )
        chance = 1.0 / (1.0 + jnp.exp2(logits * slope + level))
        corner = chance[:rows, :rows] - jnp.where(step == 0, 1.0, 0.0) * diagonal
        edge = jnp.concatenate([corner, chance[rows:, :rows]], axis=0)
        coeff = (scale * jnp.concatenate([edge, chance[:, rows:]], axis=1)).astype(BF16)
        coeff_buf[...] = coeff
        coeff_t_buf[...] = coeff.T
        image_sum[unit] += jnp.dot(coeff_buf[...], txts[h], preferred_element_type=F32)
        text_sum[h] += jnp.dot(coeff_t_buf[...], imgs[unit], preferred_element_type=F32)
        return carry

    lax.fori_loop(0, len(ORDER), tile, 0)
    act_all(CLOSING)

    for side, which, events in FINISH:
        act_all((events,))
        part = "ab".index(which)
        here = pl.ds(part * half, half)
        embed_ref, place, out_ref = {
            "image": (image_ref, own, grads_ref.at[0]),
            "text": (text_ref, txt(0, 0), grads_ref.at[1]),
        }[side]
        unit_part, inverse = unit_rows(embed_ref[here])
        direction = total(side, place, part)
        along = jnp.sum(unit_part * direction, axis=1, keepdims=True)
        out_ref[here] = (direction - unit_part * along) * inverse

    for kind, name, part in sent:
        kind(name, part).wait_send()


def per_device(picture, caption, inverse_softness, similarity_offset):
    rows, width = picture.shape
    scalar = pl.BlockSpec(memory_space=pltpu.SMEM)
    whole = pl.BlockSpec(memory_space=pltpu.VMEM)
    pairs = 15 * rows * 8 * rows
    grads = pl.pallas_call(
        kernel,
        out_shape=jax.ShapeDtypeStruct((2, rows, width), F32),
        in_specs=[scalar, scalar, whole, whole],
        out_specs=whole,
        scratch_shapes=[
            pltpu.VMEM((UNITS, 2 * rows, width), BF16),
            pltpu.VMEM((2, 4 * rows, width), BF16),
            pltpu.VMEM((UNITS, 2 * rows, width), F32),
            pltpu.VMEM((2, 4 * rows, width), F32),
            pltpu.VMEM((2 * rows, 4 * rows), BF16),
            pltpu.VMEM((4 * rows, 2 * rows), BF16),
            pltpu.VMEM((2 * MESSAGES, rows // 2, width), BF16),
            pltpu.VMEM((2 * MESSAGES, rows // 2, width), BF16),
            pltpu.SemaphoreType.DMA((4 * MESSAGES,)),
            pltpu.SemaphoreType.DMA((4 * MESSAGES,)),
        ],
        compiler_params=pltpu.CompilerParams(
            collective_id=0, has_side_effects=True, vmem_limit_bytes=56 * 2**20
        ),
        cost_estimate=pl.CostEstimate(
            flops=6 * pairs * width, bytes_accessed=16 * rows * width, transcendentals=2 * pairs
        ),
    )(inverse_softness, similarity_offset, picture, caption)
    return grads[0], grads[1]


def solution(mesh):
    spec = P(("blk", "group"), None)
    return jax.shard_map(
        per_device,
        mesh=mesh,
        in_specs=(spec, spec, P(), P()),
        out_specs=(spec, spec),
        check_vma=False,
    )
```

```python
import functools

import jax
import jax.numpy as jnp
from jax import lax
from jax.experimental import pallas as pl
from jax.experimental.pallas import tpu as pltpu
from jax.sharding import PartitionSpec as P

EPS = 1e-06
LOG2_E = 1.4426950408889634
F32 = jnp.float32
BF16 = jnp.bfloat16

UNITS = 8
MESSAGES = 24

OPENING = (
    ("+TYa", "+IYa", "+AUa", "+BUa", "+TR0a", "+TL0b", "+TYb", "+AUb", "+BUb", "+TR0b",),
    ("+TL0a", "+IC",),
)
ORDER = (
    (0, 0), (2, 0), (3, 0), (1, 0), (6, 0), (8, 0), (1, 1), (6, 1),
    (9, 0), (7, 0), (7, 1), (9, 1), (8, 1), (2, 1), (3, 1), (0, 1),
)
BEFORE = {
    0: (
        ("-TR0a", "+HR0a", "-TL0b", "+HL0b", "-TYa", "+TR1a", "+TL1a", "-AUa", "-BUa", "+MCa",),
        ("+PCa", "-IYa", "+GYa", "+ZYa", "+JYa", "-AUb", "-BUb", "+SYb", "+IYb", "+F1",),
        ("+MCb", "+PCb", "-TYb", "+TR1b", "+TL1b", "-IC", "-TR0b", "-TL0a", "-HR0a", "-HL0b",),
    ),
    1: (
        ("-GYa", "+F2a", "+KYa", "-MC", "-PC",),
    ),
    2: (
        ("-IYb", "+ZYb", "+JYb",),
    ),
    3: (
        ("-JY", "-TR1a", "+HR1a", "-TL1b", "+HL1b",),
    ),
    4: (
        ("-F1", "-SYb", "+F2b", "+KYb",),
    ),
    5: (
        ("-KY", "-ZYa", "+LYa",),
    ),
    6: (
        ("-ZYb", "+LYb", "-TR1b", "-TL1a", "-HR1a", "-HL1b",),
    ),
    7: (
        ("-F2a", "+F3a", "<JY",),
    ),
    8: (
        ("-LY", "-F2b", "+F3b", "<F1",),
    ),
    9: (
        ("-F3",),
    ),
    10: (
        ("<HR0a", "<HL0b", "<TR0b", "<TL0a",),
    ),
    11: (
        ("<F3",),
    ),
    12: (
        ("<LY", ">F3a", "<F2a", ">F3b", "<F2b",),
    ),
    13: (
        (">LY", "<ZY", "<KY",),
    ),
    14: (
        (">HR0a", "<TR0a", ">HL0b", "<TL0b", ">KY", ">F1", ">JY",),
    ),
    15: (
        ("<MC", "<PC",),
    ),
}
CLOSING = (
    ("<HR1a", "<HL1b", "<TR1b", "<TL1a", ">F2a", "<GYa", "<IC", ">MC", ">PC", "<AU",),
    ("<BUa", ">F2b", "<SYb", ">ZYb", "<IYb", ">HR1a", "<TR1a", ">HL1b", "<TL1b", ">ZYa",),
    (">GYa", "<IYa", ">SYb", "<BUb", ">TR1b", ">TL1b", "<TYb", ">TR1a", ">TL1a", "<TYa",),
    (">TR0", ">TL0", ">IC", ">AU", ">BUa",),
)
FINISH = (
    ("image", "a", (">IYa",)),
    ("image", "b", (">IYb", ">BUb")),
    ("text", "b", (">TYb",)),
    ("text", "a", (">TYa",)),
)


def unit_rows(embed):
    inverse = lax.rsqrt(jnp.sum(embed * embed, axis=1, keepdims=True) + EPS)
    return embed * inverse, inverse


def kernel(
    scale_ref,
    offset_ref,
    image_ref,
    text_ref,
    grads_ref,
    imgs,
    txts,
    image_sum,
    text_sum,
    coeff_buf,
    coeff_t_buf,
    sums_out,
    sums_in,
    grads,
    send_sem,
    recv_sem,
    out_sem,
):
    rows, width = image_ref.shape
    half = rows // 2
    n_blk = lax.axis_size("blk")
    blk = lax.axis_index("blk")
    group = lax.axis_index("group")
    core = blk % 2
    y = (blk // 2) % 2

    def device(dz=0, flip=0, dx=0, flip_y=0):
        plane = (blk // 4 + dz + n_blk // 4) % (n_blk // 4)
        within = blk % 4
        if flip % 2:
            within = within + 1 - 2 * core
        if flip // 2:
            within = within + 2 - 4 * y
        x = (group % 4 + dx + 4) % 4
        upper = group // 4
        if flip_y:
            upper = 1 - upper
        return (plane * 4 + within, upper * 4 + x)

    mate, y_near, y_far = device(flip=1), device(flip=2), device(flip_y=1)
    right, left = device(dx=1), device(dx=-1)
    cross = device(dz=2 * core - 1, flip=1)
    y_on, y_back = device(dz=1 - 2 * y), device(dz=2 * y - 1)

    barrier = pltpu.get_barrier_semaphore()
    for partner in (mate, y_near, y_on, y_back, cross, right, left, y_far):
        pl.semaphore_signal(barrier, inc=1, device_id=partner, device_id_type=pl.DeviceIdType.MESH)

    def img(unit, k=0):
        return imgs, image_sum, unit, k * rows

    def txt(h, k):
        return txts, text_sum, h, k * rows

    own, own_y, on, back_, on_y, back_y = img(0), img(1), img(2 + y), img(3 - y), img(4 + y), img(5 - y)

    routes = {
        "IY": (own, own_y, y_near, y_near),
        "IC": (own, img(0, 1), mate, mate),
        "JY": (own_y, img(1, 1), mate, mate),
        "AU": (own, on, y_on, y_back),
        "BU": (own, back_, y_back, y_on),
        "GY": (own_y, on_y, y_on, y_back),
        "SY": (back_, back_y, y_near, y_near, on_y),
        "ZY": (own_y, back_y, y_back, y_on),
        "MC": (img(2), img(2, 1), mate, mate),
        "PC": (img(3), img(3, 1), mate, mate),
        "KY": (on_y, img(4 + y, 1), mate, mate),
        "LY": (back_y, img(5 - y, 1), mate, mate),
        "F1": (img(3 - core), img(6), cross, cross),
        "F2": (on_y, img(7), y_on, y_back),
        "F3": (img(7), img(7, 1), mate, mate),
        "TY": (txt(0, 0), txt(1, 0), y_far, y_far),
    }
    for h in range(2):
        routes[f"TR{h}"] = (txt(h, 0), txt(h, 3), right, left)
        routes[f"TL{h}"] = (txt(h, 0), txt(h, 1), left, right)
        routes[f"HR{h}"] = (txt(h, 3), txt(h, 2), right, left)
        routes[f"HL{h}"] = (txt(h, 1), txt(h, 2), left, right)
    names = list(routes)
    joins = {
        "F2": ("F3",),
        "GY": ("KY", "F2"),
        "SY": ("KY", "F2"),
        "ZY": ("LY",),
        "IY": ("JY", "ZY", "GY"),
        "image": ("IC", "IY", "AU", "BU"),
        "TY": ("TR1", "TL1"),
        "text": ("TR0", "TL0", "TY"),
    }
    for h in range(2):
        joins[f"TR{h}"], joins[f"TL{h}"] = (f"HR{h}",), (f"HL{h}",)
    in_place = ("MC", "PC", "F1", "SY")
    sent, added = [], set()

    def copy(index, source, target, to):
        return pltpu.make_async_remote_copy(
            src_ref=source,
            dst_ref=target,
            send_sem=send_sem.at[index],
            recv_sem=recv_sem.at[index],
            device_id=to,
            device_id_type=pl.DeviceIdType.MESH,
        )

    def at(place, part):
        return place[2], pl.ds(place[3] + part * half, half)

    def gather(name, part):
        source, target, to = routes[name][:3]
        return copy(
            2 * names.index(name) + part, source[0].at[at(source, part)], target[0].at[at(target, part)], to
        )

    def back(name, part):
        index = 2 * names.index(name) + part
        return copy(2 * len(names) + index, sums_out.at[index], sums_in.at[index], routes[name][3])

    def total(name, place, part):
        value = place[1][at(place, part)]
        for other in joins.get(name, ()):
            if (other, part) in added:
                value = value + sums_in[2 * names.index(other) + part].astype(F32)
        return value

    def act(event):
        parts = (0, 1)
        kind, name = event[0], event[1:]
        if name[-1] in "ab":
            parts, name = ("ab".index(name[-1]),), name[:-1]
        for part in parts:
            index = 2 * names.index(name) + part
            if kind == "+":
                gather(name, part).start()
                sent.append((gather, name, part))
            elif kind == "-":
                gather(name, part).wait_recv()
            elif kind == "<":
                sums_out[index] = total(name, (routes[name] + routes[name][1:2])[4], part).astype(BF16)
                back(name, part).start()
                sent.append((back, name, part))
            else:
                back(name, part).wait_recv()
                if name in in_place:
                    place = routes[name][0]
                    place[1][at(place, part)] += sums_in[index].astype(F32)
                else:
                    added.add((name, part))

    def act_all(events):
        for line in events:
            for event in line:
                act(event)

    scale = scale_ref[0]
    offset = offset_ref[0]
    unit_image, inv_image = unit_rows(image_ref[...])
    imgs[0, :rows] = unit_image.astype(BF16)
    unit_text, inv_text = unit_rows(text_ref[...])
    txts[0, :rows] = unit_text.astype(BF16)

    pl.semaphore_wait(barrier, 8)
    act_all(OPENING)
    image_sum[...] = jnp.zeros_like(image_sum)
    text_sum[...] = jnp.zeros_like(text_sum)
    imgs[6, rows:] = jnp.zeros((rows, width), BF16)

    row = lax.broadcasted_iota(jnp.int32, (rows, rows), 0)
    column = lax.broadcasted_iota(jnp.int32, (rows, rows), 1)
    diagonal = jnp.where(row == column, 1.0, 0.0).astype(F32)
    slope, level = scale * -LOG2_E, offset * -LOG2_E

    def pick(step, values):
        picked = values[0]
        for i, value in enumerate(values[1:]):
            picked = jnp.where(step > i, value, picked)
        return picked

    def tile(step, carry):
        unit = pick(step, [{8: 4 + y, 9: 5 - y}.get(u, u) for u, _ in ORDER])
        h = pick(step, [h for _, h in ORDER])
        for when, events in BEFORE.items():
            pl.when(step == when)(functools.partial(act_all, events))

        logits = lax.dot_general(
            imgs[unit], txts[h], (((1,), (1,)), ((), ())), preferred_element_type=F32
        )
        chance = 1.0 / (1.0 + jnp.exp2(logits * slope + level))
        corner = chance[:rows, :rows] - jnp.where(step == 0, 1.0, 0.0) * diagonal
        edge = jnp.concatenate([corner, chance[rows:, :rows]], axis=0)
        coeff = (scale * jnp.concatenate([edge, chance[:, rows:]], axis=1)).astype(BF16)
        coeff_buf[...] = coeff
        coeff_t_buf[...] = coeff.T
        image_sum[unit] += jnp.dot(coeff_buf[...], txts[h], preferred_element_type=F32)
        text_sum[h] += jnp.dot(coeff_t_buf[...], imgs[unit], preferred_element_type=F32)
        return carry

    lax.fori_loop(0, len(ORDER), tile, 0)
    act_all(CLOSING)

    written = []
    for side, which, events in FINISH:
        part = "ab".index(which)
        here = pl.ds(part * half, half)
        embed_ref, place, out = {
            "image": (image_ref, own, 0),
            "text": (text_ref, txt(0, 0), 1),
        }[side]
        unit_part, inverse = unit_rows(embed_ref[here])
        act_all((events,))
        direction = total(side, place, part)
        along = jnp.sum(unit_part * direction, axis=1, keepdims=True)
        grads[out, here] = (direction - unit_part * along) * inverse
        write = pltpu.make_async_copy(
            grads.at[out, here], grads_ref.at[out, here], out_sem.at[len(written)]
        )
        write.start()
        written.append(write)

    for kind, name, part in sent:
        kind(name, part).wait_send()
    for write in written:
        write.wait()


def per_device(picture, caption, inverse_softness, similarity_offset):
    rows, width = picture.shape
    scalar = pl.BlockSpec(memory_space=pltpu.SMEM)
    whole = pl.BlockSpec(memory_space=pltpu.VMEM)
    pairs = 15 * rows * 8 * rows
    grads = pl.pallas_call(
        kernel,
        out_shape=jax.ShapeDtypeStruct((2, rows, width), F32),
        in_specs=[scalar, scalar, whole, whole],
        out_specs=pl.BlockSpec(memory_space=pl.ANY),
        scratch_shapes=[
            pltpu.VMEM((UNITS, 2 * rows, width), BF16),
            pltpu.VMEM((2, 4 * rows, width), BF16),
            pltpu.VMEM((UNITS, 2 * rows, width), F32),
            pltpu.VMEM((2, 4 * rows, width), F32),
            pltpu.VMEM((2 * rows, 4 * rows), BF16),
            pltpu.VMEM((4 * rows, 2 * rows), BF16),
            pltpu.VMEM((2 * MESSAGES, rows // 2, width), BF16),
            pltpu.VMEM((2 * MESSAGES, rows // 2, width), BF16),
            pltpu.VMEM((2, rows, width), F32),
            pltpu.SemaphoreType.DMA((4 * MESSAGES,)),
            pltpu.SemaphoreType.DMA((4 * MESSAGES,)),
            pltpu.SemaphoreType.DMA((len(FINISH),)),
        ],
        compiler_params=pltpu.CompilerParams(
            collective_id=0, has_side_effects=True, vmem_limit_bytes=56 * 2**20
        ),
        cost_estimate=pl.CostEstimate(
            flops=6 * pairs * width, bytes_accessed=16 * rows * width, transcendentals=2 * pairs
        ),
    )(inverse_softness, similarity_offset, picture, caption)
    return grads[0], grads[1]


def solution(mesh):
    spec = P(("blk", "group"), None)
    return jax.shard_map(
        per_device,
        mesh=mesh,
        in_specs=(spec, spec, P(), P()),
        out_specs=(spec, spec),
        check_vma=False,
    )
```

```python
import functools

import jax
import jax.numpy as jnp
from jax import lax
from jax.experimental import pallas as pl
from jax.experimental.pallas import tpu as pltpu
from jax.sharding import PartitionSpec as P

EPS = 1e-06
LOG2_E = 1.4426950408889634
F32 = jnp.float32
BF16 = jnp.bfloat16

UNITS = 8
MESSAGES = 24

OPENING = (
    ("+TYa", "+TR0a", "+TL0b", "+TYb", "+TR0b", "+TL0a"),
    ("+IYa", "+AUa", "+BUa", "+AUb", "+BUb", "+IC"),
)
ORDER = (
    (0, 0), (2, 0), (3, 0), (1, 0), (6, 0), (8, 0), (1, 1), (6, 1),
    (9, 0), (7, 0), (7, 1), (9, 1), (8, 1), (2, 1), (3, 1), (0, 1),
)
BEFORE = {
    0: (
        ("-TR0a", "+HR0a", "-TL0b", "+HL0b", "-TYa", "+TR1a", "+TL1a", "-AUa", "-BUa", "+MCa",),
        ("+PCa", "-IYa", "+GYa", "+ZYa", "+JYa", "-AUb", "-BUb", "+SYb", "+IYb", "+F1",),
        ("+MCb", "+PCb", "-TYb", "+TR1b", "+TL1b", "-IC", "-TR0b", "-TL0a", "-HR0a", "-HL0b",),
    ),
    1: (
        ("-GYa", "+F2a", "+KYa", "-MC", "-PC",),
    ),
    2: (
        ("-IYb", "+ZYb", "+JYb",),
    ),
    3: (
        ("-JY", "-TR1a", "+HR1a", "-TL1b", "+HL1b",),
    ),
    4: (
        ("-F1", "-SYb", "+F2b", "+KYb",),
    ),
    5: (
        ("-KY", "-ZYa", "+LYa",),
    ),
    6: (
        ("-ZYb", "+LYb", "-TR1b", "-TL1a", "-HR1a", "-HL1b",),
    ),
    7: (
        ("-F2a", "+F3a", "<JY",),
    ),
    8: (
        ("-LY", "-F2b", "+F3b", "<F1",),
    ),
    9: (
        ("-F3",),
    ),
    10: (
        ("<HR0a", "<HL0b", "<TR0b", "<TL0a",),
    ),
    11: (
        ("<F3",),
    ),
    12: (
        ("<LY", ">F3a", "<F2a", ">F3b", "<F2b",),
    ),
    13: (
        (">LY", "<ZY", "<KY",),
    ),
    14: (
        (">HR0a", "<TR0a", ">HL0b", "<TL0b", ">KY", ">F1", ">JY",),
    ),
    15: (
        ("<MC", "<PC",),
    ),
}
CLOSING = (
    ("<HR1a", "<HL1b", "<TR1b", "<TL1a", ">F2a", "<GYa", "<IC", ">MC", ">PC", "<AU",),
    ("<BUa", ">F2b", "<SYb", ">ZYb", "<IYb", ">HR1a", "<TR1a", ">HL1b", "<TL1b", ">ZYa",),
    (">GYa", "<IYa", ">SYb", "<BUb", ">TR1b", ">TL1b", "<TYb", ">TR1a", ">TL1a", "<TYa",),
    (">TR0", ">TL0", ">IC", ">AU", ">BUa",),
)
FINISH = (
    ("image", "a", (">IYa",)),
    ("image", "b", (">IYb", ">BUb")),
    ("text", "b", (">TYb",)),
    ("text", "a", (">TYa",)),
)


def unit_rows(embed):
    inverse = lax.rsqrt(jnp.sum(embed * embed, axis=1, keepdims=True) + EPS)
    return embed * inverse, inverse


def kernel(
    scale_ref,
    offset_ref,
    image_ref,
    text_ref,
    grads_ref,
    imgs,
    txts,
    image_sum,
    text_sum,
    coeff_buf,
    coeff_t_buf,
    sums_out,
    sums_in,
    grads,
    send_sem,
    recv_sem,
    out_sem,
):
    rows, width = image_ref.shape
    half = rows // 2
    n_blk = lax.axis_size("blk")
    blk = lax.axis_index("blk")
    group = lax.axis_index("group")
    core = blk % 2
    y = (blk // 2) % 2

    def device(dz=0, flip=0, dx=0, flip_y=0):
        plane = (blk // 4 + dz + n_blk // 4) % (n_blk // 4)
        within = blk % 4
        if flip % 2:
            within = within + 1 - 2 * core
        if flip // 2:
            within = within + 2 - 4 * y
        x = (group % 4 + dx + 4) % 4
        upper = group // 4
        if flip_y:
            upper = 1 - upper
        return (plane * 4 + within, upper * 4 + x)

    mate, y_near, y_far = device(flip=1), device(flip=2), device(flip_y=1)
    right, left = device(dx=1), device(dx=-1)
    cross = device(dz=2 * core - 1, flip=1)
    y_on, y_back = device(dz=1 - 2 * y), device(dz=2 * y - 1)

    barrier = pltpu.get_barrier_semaphore()
    for partner in (mate, y_near, y_on, y_back, cross, right, left, y_far):
        pl.semaphore_signal(barrier, inc=1, device_id=partner, device_id_type=pl.DeviceIdType.MESH)

    def img(unit, k=0):
        return imgs, image_sum, unit, k * rows

    def txt(h, k):
        return txts, text_sum, h, k * rows

    own, own_y, on, back_, on_y, back_y = img(0), img(1), img(2 + y), img(3 - y), img(4 + y), img(5 - y)

    routes = {
        "IY": (own, own_y, y_near, y_near),
        "IC": (own, img(0, 1), mate, mate),
        "JY": (own_y, img(1, 1), mate, mate),
        "AU": (own, on, y_on, y_back),
        "BU": (own, back_, y_back, y_on),
        "GY": (own_y, on_y, y_on, y_back),
        "SY": (back_, back_y, y_near, y_near, on_y),
        "ZY": (own_y, back_y, y_back, y_on),
        "MC": (img(2), img(2, 1), mate, mate),
        "PC": (img(3), img(3, 1), mate, mate),
        "KY": (on_y, img(4 + y, 1), mate, mate),
        "LY": (back_y, img(5 - y, 1), mate, mate),
        "F1": (img(3 - core), img(6), cross, cross),
        "F2": (on_y, img(7), y_on, y_back),
        "F3": (img(7), img(7, 1), mate, mate),
        "TY": (txt(0, 0), txt(1, 0), y_far, y_far),
    }
    for h in range(2):
        routes[f"TR{h}"] = (txt(h, 0), txt(h, 3), right, left)
        routes[f"TL{h}"] = (txt(h, 0), txt(h, 1), left, right)
        routes[f"HR{h}"] = (txt(h, 3), txt(h, 2), right, left)
        routes[f"HL{h}"] = (txt(h, 1), txt(h, 2), left, right)
    names = list(routes)
    joins = {
        "F2": ("F3",),
        "GY": ("KY", "F2"),
        "SY": ("KY", "F2"),
        "ZY": ("LY",),
        "IY": ("JY", "ZY", "GY"),
        "image": ("IC", "IY", "AU", "BU"),
        "TY": ("TR1", "TL1"),
        "text": ("TR0", "TL0", "TY"),
    }
    for h in range(2):
        joins[f"TR{h}"], joins[f"TL{h}"] = (f"HR{h}",), (f"HL{h}",)
    in_place = ("MC", "PC", "F1", "SY")
    sent, added = [], set()

    def copy(index, source, target, to):
        return pltpu.make_async_remote_copy(
            src_ref=source,
            dst_ref=target,
            send_sem=send_sem.at[index],
            recv_sem=recv_sem.at[index],
            device_id=to,
            device_id_type=pl.DeviceIdType.MESH,
        )

    def at(place, part):
        return place[2], pl.ds(place[3] + part * half, half)

    def gather(name, part):
        source, target, to = routes[name][:3]
        return copy(
            2 * names.index(name) + part, source[0].at[at(source, part)], target[0].at[at(target, part)], to
        )

    def back(name, part):
        index = 2 * names.index(name) + part
        return copy(2 * len(names) + index, sums_out.at[index], sums_in.at[index], routes[name][3])

    def total(name, place, part):
        value = place[1][at(place, part)]
        for other in joins.get(name, ()):
            if (other, part) in added:
                value = value + sums_in[2 * names.index(other) + part].astype(F32)
        return value

    def act(event):
        parts = (0, 1)
        kind, name = event[0], event[1:]
        if name[-1] in "ab":
            parts, name = ("ab".index(name[-1]),), name[:-1]
        for part in parts:
            index = 2 * names.index(name) + part
            if kind == "+":
                gather(name, part).start()
                sent.append((gather, name, part))
            elif kind == "-":
                gather(name, part).wait_recv()
            elif kind == "<":
                sums_out[index] = total(name, (routes[name] + routes[name][1:2])[4], part).astype(BF16)
                back(name, part).start()
                sent.append((back, name, part))
            else:
                back(name, part).wait_recv()
                if name in in_place:
                    place = routes[name][0]
                    place[1][at(place, part)] += sums_in[index].astype(F32)
                else:
                    added.add((name, part))

    def act_all(events):
        for line in events:
            for event in line:
                act(event)

    scale = scale_ref[0]
    offset = offset_ref[0]
    txts[0, :rows] = unit_rows(text_ref[...])[0].astype(BF16)

    pl.semaphore_wait(barrier, 8)
    act_all(OPENING[:1])
    imgs[0, :rows] = unit_rows(image_ref[...])[0].astype(BF16)
    act_all(OPENING[1:])
    image_sum[...] = jnp.zeros_like(image_sum)
    text_sum[...] = jnp.zeros_like(text_sum)
    imgs[6, rows:] = jnp.zeros((rows, width), BF16)

    row = lax.broadcasted_iota(jnp.int32, (rows, rows), 0)
    column = lax.broadcasted_iota(jnp.int32, (rows, rows), 1)
    diagonal = jnp.where(row == column, 1.0, 0.0).astype(F32)
    slope, level = scale * -LOG2_E, offset * -LOG2_E

    def pick(step, values):
        picked = values[0]
        for i, value in enumerate(values[1:]):
            picked = jnp.where(step > i, value, picked)
        return picked

    def tile(step, carry):
        unit = pick(step, [{8: 4 + y, 9: 5 - y}.get(u, u) for u, _ in ORDER])
        h = pick(step, [h for _, h in ORDER])
        for when, events in BEFORE.items():
            pl.when(step == when)(functools.partial(act_all, events))

        logits = lax.dot_general(
            imgs[unit], txts[h], (((1,), (1,)), ((), ())), preferred_element_type=F32
        )
        chance = 1.0 / (1.0 + jnp.exp2(logits * slope + level))
        corner = chance[:rows, :rows] - jnp.where(step == 0, 1.0, 0.0) * diagonal
        edge = jnp.concatenate([corner, chance[rows:, :rows]], axis=0)
        coeff = (scale * jnp.concatenate([edge, chance[:, rows:]], axis=1)).astype(BF16)
        coeff_buf[...] = coeff
        coeff_t_buf[...] = coeff.T
        image_sum[unit] += jnp.dot(coeff_buf[...], txts[h], preferred_element_type=F32)
        text_sum[h] += jnp.dot(coeff_t_buf[...], imgs[unit], preferred_element_type=F32)
        return carry

    lax.fori_loop(0, len(ORDER), tile, 0)
    act_all(CLOSING)

    written = []
    for side, which, events in FINISH:
        part = "ab".index(which)
        here = pl.ds(part * half, half)
        embed_ref, place, out = {
            "image": (image_ref, own, 0),
            "text": (text_ref, txt(0, 0), 1),
        }[side]
        unit_part, inverse = unit_rows(embed_ref[here])
        act_all((events,))
        direction = total(side, place, part)
        along = jnp.sum(unit_part * direction, axis=1, keepdims=True)
        grads[out, here] = (direction - unit_part * along) * inverse
        write = pltpu.make_async_copy(
            grads.at[out, here], grads_ref.at[out, here], out_sem.at[len(written)]
        )
        write.start()
        written.append(write)

    for kind, name, part in sent:
        kind(name, part).wait_send()
    for write in written:
        write.wait()


def per_device(picture, caption, inverse_softness, similarity_offset):
    rows, width = picture.shape
    scalar = pl.BlockSpec(memory_space=pltpu.SMEM)
    whole = pl.BlockSpec(memory_space=pltpu.VMEM)
    pairs = 15 * rows * 8 * rows
    grads = pl.pallas_call(
        kernel,
        out_shape=jax.ShapeDtypeStruct((2, rows, width), F32),
        in_specs=[scalar, scalar, whole, whole],
        out_specs=pl.BlockSpec(memory_space=pl.ANY),
        scratch_shapes=[
            pltpu.VMEM((UNITS, 2 * rows, width), BF16),
            pltpu.VMEM((2, 4 * rows, width), BF16),
            pltpu.VMEM((UNITS, 2 * rows, width), F32),
            pltpu.VMEM((2, 4 * rows, width), F32),
            pltpu.VMEM((2 * rows, 4 * rows), BF16),
            pltpu.VMEM((4 * rows, 2 * rows), BF16),
            pltpu.VMEM((2 * MESSAGES, rows // 2, width), BF16),
            pltpu.VMEM((2 * MESSAGES, rows // 2, width), BF16),
            pltpu.VMEM((2, rows, width), F32),
            pltpu.SemaphoreType.DMA((4 * MESSAGES,)),
            pltpu.SemaphoreType.DMA((4 * MESSAGES,)),
            pltpu.SemaphoreType.DMA((len(FINISH),)),
        ],
        compiler_params=pltpu.CompilerParams(
            collective_id=0, has_side_effects=True, vmem_limit_bytes=56 * 2**20
        ),
        cost_estimate=pl.CostEstimate(
            flops=6 * pairs * width, bytes_accessed=16 * rows * width, transcendentals=2 * pairs
        ),
    )(inverse_softness, similarity_offset, picture, caption)
    return grads[0], grads[1]


def solution(mesh):
    spec = P(("blk", "group"), None)
    return jax.shard_map(
        per_device,
        mesh=mesh,
        in_specs=(spec, spec, P(), P()),
        out_specs=(spec, spec),
        check_vma=False,
    )
```

```python
import functools

import jax
import jax.numpy as jnp
from jax import lax
from jax.experimental import pallas as pl
from jax.experimental.pallas import tpu as pltpu
from jax.sharding import PartitionSpec as P

EPS = 1e-06
LOG2_E = 1.4426950408889634
F32 = jnp.float32
BF16 = jnp.bfloat16

UNITS = 8
MESSAGES = 24

OPENING = (
    ("+IYa", "+AUa", "+BUa", "+TYa", "+TR0a", "+TL0b", "+TYb", "+AUb", "+BUb", "+TR0b",),
    ("+TL0a", "+IC",),
)
ORDER = (
    (0, 0), (2, 0), (3, 0), (1, 0), (6, 0), (8, 0), (1, 1), (6, 1),
    (9, 0), (7, 0), (7, 1), (9, 1), (8, 1), (2, 1), (3, 1), (0, 1),
)
BEFORE = {
    0: (
        ("-TR0a", "+HR0a", "-TL0b", "+HL0b", "-TYa", "+TR1a", "+TL1a", "-AUa", "-BUa", "+MCa",),
        ("+PCa", "-IYa", "+GYa", "+ZYa", "+JYa", "-AUb", "-BUb", "+SYb", "+IYb", "+F1",),
        ("+MCb", "+PCb", "-TYb", "+TR1b", "+TL1b", "-IC", "-TR0b", "-TL0a", "-HR0a", "-HL0b",),
    ),
    1: (
        ("-GYa", "+F2a", "+KYa", "-MC", "-PC",),
    ),
    2: (
        ("-IYb", "+ZYb", "+JYb",),
    ),
    3: (
        ("-JY", "-TR1a", "+HR1a", "-TL1b", "+HL1b",),
    ),
    4: (
        ("-F1", "-SYb", "+F2b", "+KYb",),
    ),
    5: (
        ("-KY", "-ZYa", "+LYa",),
    ),
    6: (
        ("-ZYb", "+LYb", "-TR1b", "-TL1a", "-HR1a", "-HL1b",),
    ),
    7: (
        ("-F2a", "+F3a", "<JY",),
    ),
    8: (
        ("-LY", "-F2b", "+F3b", "<F1",),
    ),
    9: (
        ("-F3",),
    ),
    10: (
        ("<HR0a", "<HL0b", "<TR0b", "<TL0a",),
    ),
    11: (
        ("<F3",),
    ),
    12: (
        ("<LY", ">F3a", "<F2a", ">F3b", "<F2b",),
    ),
    13: (
        (">LY", "<ZY", "<KY",),
    ),
    14: (
        (">HR0a", "<TR0a", ">HL0b", "<TL0b", ">KY", ">F1", ">JY",),
    ),
    15: (
        ("<MC", "<PC",),
    ),
}
CLOSING = (
    ("<HR1a", "<HL1b", "<TR1b", "<TL1a", ">F2a", "<GYa", "<IC", ">MC", ">PC", "<AU",),
    ("<BUa", ">F2b", "<SYb", ">ZYb", "<IYb", ">HR1a", "<TR1a", ">HL1b", "<TL1b", ">ZYa",),
    (">GYa", "<IYa", ">SYb", "<BUb", ">TR1b", ">TL1b", "<TYb", ">TR1a", ">TL1a", "<TYa",),
    (">TR0", ">TL0", ">IC", ">AU", ">BUa",),
)
FINISH = (
    ("image", "a", (">IYa",)),
    ("image", "b", (">IYb", ">BUb")),
    ("text", "b", (">TYb",)),
    ("text", "a", (">TYa",)),
)


def unit_rows(embed):
    inverse = lax.rsqrt(jnp.sum(embed * embed, axis=1, keepdims=True) + EPS)
    return embed * inverse, inverse


def kernel(
    scale_ref,
    offset_ref,
    image_ref,
    text_ref,
    grads_ref,
    imgs,
    txts,
    image_sum,
    text_sum,
    coeff_buf,
    coeff_t_buf,
    sums_out,
    sums_in,
    grads,
    send_sem,
    recv_sem,
    out_sem,
):
    rows, width = image_ref.shape
    half = rows // 2
    n_blk = lax.axis_size("blk")
    blk = lax.axis_index("blk")
    group = lax.axis_index("group")
    core = blk % 2
    y = (blk // 2) % 2

    def device(dz=0, flip=0, dx=0, flip_y=0):
        plane = (blk // 4 + dz + n_blk // 4) % (n_blk // 4)
        within = blk % 4
        if flip % 2:
            within = within + 1 - 2 * core
        if flip // 2:
            within = within + 2 - 4 * y
        x = (group % 4 + dx + 4) % 4
        upper = group // 4
        if flip_y:
            upper = 1 - upper
        return (plane * 4 + within, upper * 4 + x)

    mate, y_near, y_far = device(flip=1), device(flip=2), device(flip_y=1)
    right, left = device(dx=1), device(dx=-1)
    cross = device(dz=2 * core - 1, flip=1)
    y_on, y_back = device(dz=1 - 2 * y), device(dz=2 * y - 1)

    barrier = pltpu.get_barrier_semaphore()
    for partner in (mate, y_near, y_on, y_back, cross, right, left, y_far):
        pl.semaphore_signal(barrier, inc=1, device_id=partner, device_id_type=pl.DeviceIdType.MESH)

    def img(unit, k=0):
        return imgs, image_sum, unit, k * rows

    def txt(h, k):
        return txts, text_sum, h, k * rows

    own, own_y, on, back_, on_y, back_y = img(0), img(1), img(2 + y), img(3 - y), img(4 + y), img(5 - y)

    routes = {
        "IY": (own, own_y, y_near, y_near),
        "IC": (own, img(0, 1), mate, mate),
        "JY": (own_y, img(1, 1), mate, mate),
        "AU": (own, on, y_on, y_back),
        "BU": (own, back_, y_back, y_on),
        "GY": (own_y, on_y, y_on, y_back),
        "SY": (back_, back_y, y_near, y_near, on_y),
        "ZY": (own_y, back_y, y_back, y_on),
        "MC": (img(2), img(2, 1), mate, mate),
        "PC": (img(3), img(3, 1), mate, mate),
        "KY": (on_y, img(4 + y, 1), mate, mate),
        "LY": (back_y, img(5 - y, 1), mate, mate),
        "F1": (img(3 - core), img(6), cross, cross),
        "F2": (on_y, img(7), y_on, y_back),
        "F3": (img(7), img(7, 1), mate, mate),
        "TY": (txt(0, 0), txt(1, 0), y_far, y_far),
    }
    for h in range(2):
        routes[f"TR{h}"] = (txt(h, 0), txt(h, 3), right, left)
        routes[f"TL{h}"] = (txt(h, 0), txt(h, 1), left, right)
        routes[f"HR{h}"] = (txt(h, 3), txt(h, 2), right, left)
        routes[f"HL{h}"] = (txt(h, 1), txt(h, 2), left, right)
    names = list(routes)
    joins = {
        "F2": ("F3",),
        "GY": ("KY", "F2"),
        "SY": ("KY", "F2"),
        "ZY": ("LY",),
        "IY": ("JY", "ZY", "GY"),
        "image": ("IC", "IY", "AU", "BU"),
        "TY": ("TR1", "TL1"),
        "text": ("TR0", "TL0", "TY"),
    }
    for h in range(2):
        joins[f"TR{h}"], joins[f"TL{h}"] = (f"HR{h}",), (f"HL{h}",)
    in_place = ("MC", "PC", "F1", "SY")
    sent, added = [], set()

    def copy(index, source, target, to):
        return pltpu.make_async_remote_copy(
            src_ref=source,
            dst_ref=target,
            send_sem=send_sem.at[index],
            recv_sem=recv_sem.at[index],
            device_id=to,
            device_id_type=pl.DeviceIdType.MESH,
        )

    def at(place, part):
        return place[2], pl.ds(place[3] + part * half, half)

    def gather(name, part):
        source, target, to = routes[name][:3]
        return copy(
            2 * names.index(name) + part, source[0].at[at(source, part)], target[0].at[at(target, part)], to
        )

    def back(name, part):
        index = 2 * names.index(name) + part
        return copy(2 * len(names) + index, sums_out.at[index], sums_in.at[index], routes[name][3])

    def total(name, place, part):
        value = place[1][at(place, part)]
        for other in joins.get(name, ()):
            if (other, part) in added:
                value = value + sums_in[2 * names.index(other) + part].astype(F32)
        return value

    def act(event):
        parts = (0, 1)
        kind, name = event[0], event[1:]
        if name[-1] in "ab":
            parts, name = ("ab".index(name[-1]),), name[:-1]
        for part in parts:
            index = 2 * names.index(name) + part
            if kind == "+":
                gather(name, part).start()
                sent.append((gather, name, part))
            elif kind == "-":
                gather(name, part).wait_recv()
            elif kind == "<":
                sums_out[index] = total(name, (routes[name] + routes[name][1:2])[4], part).astype(BF16)
                back(name, part).start()
                sent.append((back, name, part))
            else:
                back(name, part).wait_recv()
                if name in in_place:
                    place = routes[name][0]
                    place[1][at(place, part)] += sums_in[index].astype(F32)
                else:
                    added.add((name, part))

    def act_all(events):
        for line in events:
            for event in line:
                act(event)

    scale = scale_ref[0]
    offset = offset_ref[0]
    unit_image, inv_image = unit_rows(image_ref[...])
    imgs[0, :rows] = unit_image.astype(BF16)
    unit_text, inv_text = unit_rows(text_ref[...])
    txts[0, :rows] = unit_text.astype(BF16)

    pl.semaphore_wait(barrier, 8)
    act_all(OPENING)
    image_sum[...] = jnp.zeros_like(image_sum)
    text_sum[...] = jnp.zeros_like(text_sum)
    imgs[6, rows:] = jnp.zeros((rows, width), BF16)

    row = lax.broadcasted_iota(jnp.int32, (rows, rows), 0)
    column = lax.broadcasted_iota(jnp.int32, (rows, rows), 1)
    diagonal = jnp.where(row == column, 1.0, 0.0).astype(F32)
    slope, level = scale * -LOG2_E, offset * -LOG2_E

    def pick(step, values):
        picked = values[0]
        for i, value in enumerate(values[1:]):
            picked = jnp.where(step > i, value, picked)
        return picked

    def tile(step, carry):
        unit = pick(step, [{8: 4 + y, 9: 5 - y}.get(u, u) for u, _ in ORDER])
        h = pick(step, [h for _, h in ORDER])
        for when, events in BEFORE.items():
            pl.when(step == when)(functools.partial(act_all, events))

        logits = lax.dot_general(
            imgs[unit], txts[h], (((1,), (1,)), ((), ())), preferred_element_type=F32
        )
        chance = 1.0 / (1.0 + jnp.exp2(logits * slope + level))
        corner = chance[:rows, :rows] - jnp.where(step == 0, 1.0, 0.0) * diagonal
        edge = jnp.concatenate([corner, chance[rows:, :rows]], axis=0)
        coeff = (scale * jnp.concatenate([edge, chance[:, rows:]], axis=1)).astype(BF16)
        coeff_buf[...] = coeff
        coeff_t_buf[...] = coeff.T
        image_sum[unit] += jnp.dot(coeff_buf[...], txts[h], preferred_element_type=F32)
        text_sum[h] += jnp.dot(coeff_t_buf[...], imgs[unit], preferred_element_type=F32)
        return carry

    lax.fori_loop(0, len(ORDER), tile, 0)
    act_all(CLOSING)

    written = []
    for side, which, events in FINISH:
        part = "ab".index(which)
        here = pl.ds(part * half, half)
        embed_ref, place, out = {
            "image": (image_ref, own, 0),
            "text": (text_ref, txt(0, 0), 1),
        }[side]
        unit_part, inverse = unit_rows(embed_ref[here])
        act_all((events,))
        direction = total(side, place, part)
        along = jnp.sum(unit_part * direction, axis=1, keepdims=True)
        grads[out, here] = (direction - unit_part * along) * inverse
        write = pltpu.make_async_copy(
            grads.at[out, here], grads_ref.at[out, here], out_sem.at[len(written)]
        )
        write.start()
        written.append(write)

    for kind, name, part in sent:
        kind(name, part).wait_send()
    for write in written:
        write.wait()


def per_device(picture, caption, inverse_softness, similarity_offset):
    rows, width = picture.shape
    scalar = pl.BlockSpec(memory_space=pltpu.SMEM)
    whole = pl.BlockSpec(memory_space=pltpu.VMEM)
    pairs = 15 * rows * 8 * rows
    grads = pl.pallas_call(
        kernel,
        out_shape=jax.ShapeDtypeStruct((2, rows, width), F32),
        in_specs=[scalar, scalar, whole, whole],
        out_specs=pl.BlockSpec(memory_space=pl.ANY),
        scratch_shapes=[
            pltpu.VMEM((UNITS, 2 * rows, width), BF16),
            pltpu.VMEM((2, 4 * rows, width), BF16),
            pltpu.VMEM((UNITS, 2 * rows, width), F32),
            pltpu.VMEM((2, 4 * rows, width), F32),
            pltpu.VMEM((2 * rows, 4 * rows), BF16),
            pltpu.VMEM((4 * rows, 2 * rows), BF16),
            pltpu.VMEM((2 * MESSAGES, rows // 2, width), BF16),
            pltpu.VMEM((2 * MESSAGES, rows // 2, width), BF16),
            pltpu.VMEM((2, rows, width), F32),
            pltpu.SemaphoreType.DMA((4 * MESSAGES,)),
            pltpu.SemaphoreType.DMA((4 * MESSAGES,)),
            pltpu.SemaphoreType.DMA((len(FINISH),)),
        ],
        compiler_params=pltpu.CompilerParams(
            collective_id=0, has_side_effects=True, vmem_limit_bytes=56 * 2**20
        ),
        cost_estimate=pl.CostEstimate(
            flops=6 * pairs * width, bytes_accessed=16 * rows * width, transcendentals=2 * pairs
        ),
    )(inverse_softness, similarity_offset, picture, caption)
    return grads[0], grads[1]


def solution(mesh):
    spec = P(("blk", "group"), None)
    return jax.shard_map(
        per_device,
        mesh=mesh,
        in_specs=(spec, spec, P(), P()),
        out_specs=(spec, spec),
        check_vma=False,
    )
```
